128 devices in a mesh: gx: 16 (over z, y), gy: 8 (over x, core).
Axes of the slice: x: 4, y: 4, z: 4, core: 2. Of those that a mesh axis runs over, the one named last changes fastest.
Arguments:
- latent: bfloat16 [512, 64, 8, 128], P('gx', 'gy'), may hold values from -6 to 6
- position: bfloat16 [512, 64, 3, 8], P('gx', 'gy'), may hold values from 0 to 1
- counts: int32 [512, 64], P('gx', 'gy'), may hold values from 0 to 8, as said below
- leaving: int32 [16, 8, 9, 64], P('gx', 'gy'), may hold values from -1 to 2047, as said below
- landing: int32 [16, 8, 9, 64], P('gx', 'gy'), may hold values from -1 to 2047, as said below
- cotangent: bfloat16 [512, 64, 8, 128], P('gx', 'gy'), may hold values from -6 to 6
- encoder_weight: float32 [4, 128], replicated, may hold values from -1.5 to 1.5
- encoder_bias: float32 [128], replicated, may hold values from -3 to 3
- receiver_weight: bfloat16 [128, 128], replicated, may hold values from -0.3125 to 0.3125
- sender_weight: bfloat16 [128, 128], replicated, may hold values from -0.3125 to 0.3125
- edge_weight: bfloat16 [128, 128], replicated, may hold values from -0.3125 to 0.3125
- edge_bias: float32 [128], replicated, may hold values from -3 to 3
- message_weight: bfloat16 [128, 128], replicated, may hold values from -0.5 to 0.5
- message_bias: float32 [128], replicated, may hold values from -3 to 3
- node_weight: bfloat16 [128, 128], replicated, may hold values from -0.375 to 0.375
- summed_weight: bfloat16 [128, 128], replicated, may hold values from -0.09375 to 0.09375
- node_bias: float32 [128], replicated, may hold values from -3 to 3
- output_weight: bfloat16 [128, 128], replicated, may hold values from -0.5 to 0.5
- output_bias: float32 [128], replicated, may hold values from -3 to 3
- norm_gain: float32 [128], replicated, may hold values from 0.1 to 1.9
Outputs:
- new_latent: bfloat16 [512, 64, 8, 128], P('gx', 'gy')
- latent_grad: float32 [512, 64, 8, 128], P('gx', 'gy')
The draws below stay inside these ranges and needn't reach their ends.
Inputs may be any that keep to these rules, and one draw needn't show every extreme that they name: `counts`: particles in each cell; some cell holds exactly 8. `leaving`: entry m of direction k of a device names a slot of that device (in the order of the first step) whose particle moves to the device dx = k // 3 - 1, dy = k % 3 - 1 blocks away, periodically; k = 4 keeps it on the device; -1 marks an empty entry; the slots named by one device are distinct; some device fills all 64 entries of some direction. `landing`: entry m of direction k of a device names the slot of that device that receives the particle sent as entry m of direction k by the device dx, dy blocks back; it is -1 exactly where that sender's entry is -1; the slots named by one device are distinct.
All inputs are finite; a program needn't handle non-finite values.
Results may differ from the reference program's by a relative error of at most 0.006.
Values may be sent and summed in bfloat16 or wider, within the bound.
A program may use at most 64 MiB of HBM per device.

```python
import jax
import jax.numpy as jnp
from jax import lax

H = 128
P_SIZE = 8
CX = 32
CY = 8
M = 64
SLOTS = 2048
BLOCKS_X = 16
BLOCKS_Y = 8
NX = 512
NY = 64


def migration_plan(key):
    count_key, send_key, land_key, full_key = jax.random.split(key, 4)
    live_count = jax.random.randint(count_key, (BLOCKS_X, BLOCKS_Y, 9), M // 3, M + 1)
    full_keys = jax.random.split(full_key, 3)
    chosen_x = jax.random.randint(full_keys[0], (), 0, BLOCKS_X)
    chosen_y = jax.random.randint(full_keys[1], (), 0, BLOCKS_Y)
    chosen_k = jax.random.randint(full_keys[2], (), 0, 9)
    live_count = live_count.at[chosen_x, chosen_y, chosen_k].set(M)
    entry_order = jnp.arange(M)
    shuffle = jax.vmap(lambda part_key: jax.random.permutation(part_key, SLOTS)[:9 * M])
    outgoing = shuffle(jax.random.split(send_key, BLOCKS_X * BLOCKS_Y)).reshape(BLOCKS_X, BLOCKS_Y, 9, M)
    incoming = shuffle(jax.random.split(land_key, BLOCKS_X * BLOCKS_Y)).reshape(BLOCKS_X, BLOCKS_Y, 9, M)
    live_in = jnp.stack([jnp.roll(live_count[:, :, direction], (direction // 3 - 1, direction % 3 - 1), axis=(0, 1)) for direction in range(9)], axis=2)
    leaving = jnp.where(entry_order < live_count[..., None], outgoing, -1)
    landing = jnp.where(entry_order < live_in[..., None], incoming, -1)
    return (leaving.astype(jnp.int32), landing.astype(jnp.int32))


def draw_leaving(key, part):
    plan = migration_plan(key)
    return plan[0]


def draw_landing(key, part):
    plan = migration_plan(key)
    return plan[1]


def draw_counts(key, part):
    key = jax.random.fold_in(key, 11)
    first_key, second_key, third_key, fourth_key = jax.random.split(key, 4)
    drawn = jax.random.randint(first_key, (NX, NY), 3 * P_SIZE // 8, P_SIZE + 1)
    packed_cell = jax.random.randint(second_key, (NX, NY), 0, 16) == 0
    counts = jnp.where(packed_cell, P_SIZE, drawn)
    corner_x = jax.random.randint(third_key, (), 0, NX)
    corner_y = jax.random.randint(fourth_key, (), 0, NY)
    counts = counts.at[corner_x, corner_y].set(P_SIZE)
    return counts.astype(jnp.int32)


def steps_of(key, dims, pieces, low, largest):
    factor_of, own = 1.0, jax.random.fold_in(key, 6)
    for axis_at, blocks in pieces:
        draws = jnp.exp(jax.random.uniform(jax.random.fold_in(own, axis_at), (blocks,), jnp.float32, low / len(pieces), largest / len(pieces)))
        factor_of = factor_of * jnp.repeat(draws, dims[axis_at] // blocks).reshape([-1 if axis == axis_at else 1 for axis in range(len(dims))])
    return factor_of


def gaussian(rng, extent, spread, reach, shards=(), kind=jnp.bfloat16):
    array = spread * jax.random.normal(rng, extent, jnp.float32)
    if shards:
        array = array * steps_of(rng, extent, shards, -0.22, 0.18)
    return jnp.clip(array, -reach, reach).astype(kind)


def setup_inputs(seed: int = 0) -> dict:
    key_list = jax.random.split(jax.random.key(seed), 21)
    return {
        "latent": gaussian(key_list[0], (NX, NY, P_SIZE, H), 1.0, 6.0, ((0, 16), (1, 8))),
        "position": jnp.clip(1.0 * jax.random.uniform(key_list[1], (NX, NY, 3, P_SIZE), jnp.float32) ** steps_of(key_list[1], (NX, NY, 3, P_SIZE), ((0, 16), (1, 8)), -0.2, 0.2), 0.0, 1.0).astype(jnp.bfloat16),
        "counts": draw_counts(jax.random.fold_in(key_list[20], 71), 0),
        "leaving": draw_leaving(jax.random.fold_in(key_list[20], 71), 0),
        "landing": draw_landing(jax.random.fold_in(key_list[20], 71), 0),
        "cotangent": gaussian(key_list[5], (NX, NY, P_SIZE, H), 1.0, 6.0, ((0, 16), (1, 8))),
        "encoder_weight": gaussian(key_list[6], (4, H), 16 ** -0.5, 1.5, (), jnp.float32),
        "encoder_bias": gaussian(key_list[7], (H,), 0.5, 3.0, (), jnp.float32),
        "receiver_weight": gaussian(key_list[8], (H, H), (3 * H) ** -0.5, 0.3125),
        "sender_weight": gaussian(key_list[9], (H, H), (3 * H) ** -0.5, 0.3125),
        "edge_weight": gaussian(key_list[10], (H, H), (3 * H) ** -0.5, 0.3125),
        "edge_bias": gaussian(key_list[11], (H,), 0.5, 3.0, (), jnp.float32),
        "message_weight": gaussian(key_list[12], (H, H), H ** -0.5, 0.5),
        "message_bias": gaussian(key_list[13], (H,), 0.5, 3.0, (), jnp.float32),
        "node_weight": gaussian(key_list[14], (H, H), (2 * H) ** -0.5, 0.375),
        "summed_weight": gaussian(key_list[15], (H, H), (32 * H) ** -0.5, 0.09375),
        "node_bias": gaussian(key_list[16], (H,), 0.5, 3.0, (), jnp.float32),
        "output_weight": gaussian(key_list[17], (H, H), H ** -0.5, 0.5),
        "output_bias": gaussian(key_list[18], (H,), 0.5, 3.0, (), jnp.float32),
        "norm_gain": jnp.clip(1.0 + 0.18 * jax.random.normal(key_list[19], (H,), jnp.float32), 0.1, 1.9),
    }


ln_eps = 1e-05

def silu_grad(values):
    sigmoid = jax.nn.sigmoid(values)
    return sigmoid * (1.0 + values * (1.0 - sigmoid))

def stencil_stack(rows_three, width_y):
    return jnp.stack([rows_three[step_x, step_y:step_y + width_y] for step_x in range(3) for step_y in range(3)], axis=1)

def edge_inputs(row_index, wide_geometry, wide_sender, receiver_proj, encoder_weight, encoder_bias, edge_weight, edge_bias):
    width_y = receiver_proj.shape[1]
    slot_count = receiver_proj.shape[2]
    latent_width = receiver_proj.shape[3]
    place_rows = lax.dynamic_slice_in_dim(wide_geometry, row_index, 3, 0).astype(jnp.float32)
    near_place = stencil_stack(place_rows, width_y)
    own_place = place_rows[1, 1:width_y + 1]
    direction = jnp.arange(9)
    offset_x = (direction // 3 - 1).astype(jnp.float32)[None, None, :, None]
    offset_y = (direction % 3 - 1).astype(jnp.float32)[None, None, :, None]
    reach_x = offset_x + near_place[:, None, :, 0, :] - own_place[:, 0, :, None, None]
    reach_y = offset_y + near_place[:, None, :, 1, :] - own_place[:, 1, :, None, None]
    reach_z = near_place[:, None, :, 2, :] - own_place[:, 2, :, None, None]
    features = (reach_x, reach_y, reach_z, reach_x * reach_x + reach_y * reach_y + reach_z * reach_z)
    encoded = encoder_bias
    for feature_index in range(4):
        encoded = encoded + features[feature_index][..., None] * encoder_weight[feature_index]
    encoded = jax.nn.relu(encoded).astype(jnp.bfloat16)
    slot_order = jnp.arange(slot_count)
    itself = (direction[None, None, :, None] == 4) & (slot_order[None, :, None, None] == slot_order[None, None, None, :])
    edge_mask = jnp.where(itself, 0.0, near_place[:, None, :, 3, :])
    sender_rows = stencil_stack(lax.dynamic_slice_in_dim(wide_sender, row_index, 3, 0), width_y)
    receiver_row = lax.dynamic_index_in_dim(receiver_proj, row_index, 0, keepdims=False)
    projected = jnp.dot(encoded.reshape(-1, latent_width), edge_weight, preferred_element_type=jnp.float32)
    projected = projected.reshape(width_y, slot_count, 9, slot_count, latent_width)
    before = projected + receiver_row[:, :, None, None, :] + sender_rows[:, None] + edge_bias
    return (encoded, before, edge_mask)

def forward_row(row_index, wide_geometry, wide_sender, receiver_proj, encoder_weight, encoder_bias, edge_weight, edge_bias, message_weight, message_bias):
    encoded, before, edge_mask = edge_inputs(row_index, wide_geometry, wide_sender, receiver_proj, encoder_weight, encoder_bias, edge_weight, edge_bias)
    latent_width = before.shape[-1]
    hidden = jax.nn.silu(before).astype(jnp.bfloat16)
    message = encoded.astype(jnp.float32) + jnp.dot(hidden.reshape(-1, latent_width), message_weight, preferred_element_type=jnp.float32).reshape(before.shape) + message_bias
    return lax.optimization_barrier(jnp.sum(edge_mask[..., None] * message, axis=(2, 3)))

def gradient_sweep(wide_geometry, wide_sender, receiver_proj, pull_back, encoder_weight, encoder_bias, edge_weight, edge_bias):
    rows_x = receiver_proj.shape[0]

    def advance(row_index):
        encoded, before, edge_mask = edge_inputs(row_index, wide_geometry, wide_sender, receiver_proj, encoder_weight, encoder_bias, edge_weight, edge_bias)
        pull_row = lax.dynamic_index_in_dim(pull_back, row_index, 0, keepdims=False)
        slope_term = edge_mask[..., None] * pull_row[:, :, None, None, :] * silu_grad(before)
        return (lax.optimization_barrier(jnp.sum(slope_term, axis=(2, 3))), lax.optimization_barrier(jnp.sum(slope_term, axis=1)))
    receive_total, into_sender = lax.map(advance, jnp.arange(rows_x, dtype=jnp.int32))
    send_total = None
    for step_x in range(3):
        for step_y in range(3):
            term = jnp.pad(into_sender[:, :, 3 * step_x + step_y], ((step_x, 2 - step_x), (step_y, 2 - step_y), (0, 0), (0, 0)))
            send_total = term if send_total is None else send_total + term
    return (send_total, receive_total)

def node_section(relocated, summed, occupied, cotangent, node_weight, summed_weight, node_bias, output_weight, output_bias, norm_gain, message_weight):
    latent_width = relocated.shape[-1]
    flat_latent = relocated.reshape(-1, latent_width)
    flat_summed = summed.astype(jnp.bfloat16).reshape(-1, latent_width)
    occupancy = occupied.reshape(-1, 1).astype(jnp.float32)
    node_inner = jnp.dot(flat_latent, node_weight, preferred_element_type=jnp.float32) + jnp.dot(flat_summed, summed_weight, preferred_element_type=jnp.float32) + node_bias
    active = jax.nn.silu(node_inner).astype(jnp.bfloat16)
    output = jnp.dot(active, output_weight, preferred_element_type=jnp.float32) + output_bias
    centred = output - lax.optimization_barrier(jnp.mean(output, axis=-1, keepdims=True))
    inv_scale = lax.rsqrt(lax.optimization_barrier(jnp.mean(centred * centred, axis=-1, keepdims=True)) + ln_eps)
    normed = centred * inv_scale
    updated = (flat_latent.astype(jnp.float32) + occupancy * normed * norm_gain).astype(jnp.bfloat16)
    grad_norm = occupancy * cotangent.reshape(-1, latent_width).astype(jnp.float32) * norm_gain
    grad_output = ((grad_norm - lax.optimization_barrier(jnp.mean(grad_norm, axis=-1, keepdims=True)) - normed * lax.optimization_barrier(jnp.mean(grad_norm * normed, axis=-1, keepdims=True))) * inv_scale).astype(jnp.bfloat16)
    grad_active = jnp.dot(grad_output, output_weight.T, preferred_element_type=jnp.float32)
    grad_inner = (grad_active * silu_grad(node_inner)).astype(jnp.bfloat16)
    grad_summed = jnp.dot(grad_inner, summed_weight.T, preferred_element_type=jnp.float32).astype(jnp.bfloat16)
    grad_self = jnp.dot(grad_inner, node_weight.T, preferred_element_type=jnp.float32)
    pull_back = jnp.dot(grad_summed, message_weight.T, preferred_element_type=jnp.float32)
    return (updated.reshape(relocated.shape), grad_self, pull_back.reshape(relocated.shape))

def finish(cotangent, grad_self, receive_total, send_core, receiver_weight, sender_weight):
    latent_width = cotangent.shape[-1]
    gradient = cotangent.reshape(-1, latent_width).astype(jnp.float32) + grad_self
    gradient = gradient + jnp.dot(receive_total.astype(jnp.bfloat16).reshape(-1, latent_width), receiver_weight.T, preferred_element_type=jnp.float32)
    gradient = gradient + jnp.dot(send_core.astype(jnp.bfloat16).reshape(-1, latent_width), sender_weight.T, preferred_element_type=jnp.float32)
    return gradient.reshape(cotangent.shape)

def move_rows(latent, leaving, landing):
    blocks = latent.reshape(BLOCKS_X, CX, BLOCKS_Y, CY, P_SIZE, H).transpose(0, 2, 1, 3, 4, 5).reshape(BLOCKS_X, BLOCKS_Y, SLOTS, H)
    picker = jax.vmap(jax.vmap(lambda block_rows, chosen: block_rows[chosen]))
    picked = picker(blocks, jnp.clip(leaving, 0, SLOTS - 1).reshape(BLOCKS_X, BLOCKS_Y, 9 * M))
    picked = jnp.where((leaving >= 0).reshape(BLOCKS_X, BLOCKS_Y, 9 * M, 1), picked, jnp.zeros_like(picked))
    picked = picked.reshape(BLOCKS_X, BLOCKS_Y, 9, M, H)
    arrived = jnp.stack([jnp.roll(picked[:, :, direction], (direction // 3 - 1, direction % 3 - 1), axis=(0, 1)) for direction in range(9)], axis=2)
    target = jnp.where(landing >= 0, landing, SLOTS).reshape(BLOCKS_X, BLOCKS_Y, 9 * M)
    placer = jax.vmap(jax.vmap(lambda block_rows, target_slots, rows_in: block_rows.at[target_slots].set(rows_in, mode='drop')))
    relocated = placer(blocks, target, arrived.reshape(BLOCKS_X, BLOCKS_Y, 9 * M, H))
    return relocated.reshape(BLOCKS_X, BLOCKS_Y, CX, CY, P_SIZE, H).transpose(0, 2, 1, 3, 4, 5).reshape(NX, NY, P_SIZE, H)

def fold_rim(wide_total):
    middle_rows = wide_total[1:-1]
    middle_rows = middle_rows.at[-1].add(wide_total[0]).at[0].add(wide_total[-1])
    core = middle_rows[:, 1:-1]
    core = core.at[:, -1].add(middle_rows[:, 0]).at[:, 0].add(middle_rows[:, -1])
    return core

def reference(latent, position, counts, leaving, landing, cotangent, encoder_weight, encoder_bias, receiver_weight, sender_weight, edge_weight, edge_bias, message_weight, message_bias, node_weight, summed_weight, node_bias, output_weight, output_bias, norm_gain):
    relocated = move_rows(latent, leaving, landing)
    occupied = (jnp.arange(P_SIZE)[None, None, :] < counts[:, :, None]).astype(jnp.bfloat16)
    geometry = jnp.concatenate([position, occupied[:, :, None, :]], axis=2)
    padding = ((1, 1), (1, 1), (0, 0), (0, 0))
    wide_latent = jnp.pad(relocated, padding, mode='wrap')
    wide_geometry = jnp.pad(geometry, padding, mode='wrap')
    wide_sender = jnp.dot(wide_latent.reshape(-1, H), sender_weight, preferred_element_type=jnp.float32).reshape(NX + 2, NY + 2, P_SIZE, H)
    receiver_proj = jnp.dot(relocated.reshape(-1, H), receiver_weight, preferred_element_type=jnp.float32).reshape(NX, NY, P_SIZE, H)
    summed = lax.map(lambda row_index: forward_row(row_index, wide_geometry, wide_sender, receiver_proj, encoder_weight, encoder_bias, edge_weight, edge_bias, message_weight, message_bias), jnp.arange(NX, dtype=jnp.int32))
    updated, grad_self, pull_back = node_section(relocated, summed, occupied, cotangent, node_weight, summed_weight, node_bias, output_weight, output_bias, norm_gain, message_weight)
    send_total, receive_total = gradient_sweep(wide_geometry, wide_sender, receiver_proj, pull_back, encoder_weight, encoder_bias, edge_weight, edge_bias)
    send_core = fold_rim(send_total)
    latent_grad = finish(cotangent, grad_self, receive_total, send_core, receiver_weight, sender_weight)
    return (updated, latent_grad)
```

```python
import jax
import jax.numpy as jnp
from jax import lax
from jax.experimental import pallas as pl
from jax.experimental.pallas import tpu as pltpu
from jax.sharding import PartitionSpec as P

ln_eps = 1e-05
F32 = jnp.float32
BF = jnp.bfloat16
BIG_PRE = 4096.0
BIG_H = 131072.0
NH = 18
GROUP = 2


def mm(a, b):
    return jnp.dot(a, b, preferred_element_type=F32)


def mmt(a, b):
    return lax.dot_general(a, b, (((1,), (1,)), ((), ())), preferred_element_type=F32)


def iota(shape, dim):
    return lax.broadcasted_iota(jnp.int32, shape, dim)


def tree(parts):
    parts = list(parts)
    while len(parts) > 1:
        parts = [
            parts[i] + parts[i + 1] if i + 1 < len(parts) else parts[i]
            for i in range(0, len(parts), 2)
        ]
    return parts[0]


def step_of(n):
    return n // 3, n % 3


def edge_kernel(
    wl_ref, geom_ref, cot_ref, ew_ref, eb_ref, rw_ref, sw_ref, dw_ref, db_ref, mw_ref, mb_ref,
    nw_ref, uw_ref, nb_ref, ow_ref, ob_ref, gain_ref,
    upd_ref, grad_ref, send_ref,
    gj_ref, gi_ref, s_ref, r_ref, rel_ref, occ_ref, cnt_ref, w1_ref, bd_ref,
    se_ref, sh_ref, sg_ref, pull_ref, acc_ref, g_ref,
):
    lane = iota((128, 128), 1)
    row = iota((128, 128), 0)
    whole = ew_ref[...]
    high = whole.astype(BF).astype(F32)
    low = whole - high
    bias_high = eb_ref[...].astype(BF).astype(F32)
    bias_low = eb_ref[...] - bias_high
    wide = lambda v: jnp.broadcast_to(v, (8, 128))
    blocks = [wide(high[c : c + 1]) for c in range(3)]
    blocks += [wide(low[c : c + 1]) for c in range(3)]
    blocks += [wide(high[3:4])] * 3 + [wide(low[3:4])] * 3
    blocks += [wide(bias_high), wide(bias_low)]
    blocks += [jnp.ones((16, 128), F32)]
    stacked = jnp.concatenate(blocks, axis=0)
    for p in range(8):
        w1_ref[:, p * 128 : (p + 1) * 128] = jnp.where(row % 8 == p, stacked, 0.0).astype(BF)
    half_w = (dw_ref[...].astype(F32) * 0.5).astype(BF)
    bd_ref[...] = jnp.zeros((256, 256), BF)
    bd_ref[0:128, 0:128] = half_w
    bd_ref[128:256, 128:256] = half_w

    comp = row // 8
    slot = row % 8
    blk = lane // 8
    in_p = lane % 8
    is_pos = blk < 12
    sel_j = jnp.where(
        is_pos & (comp == blk % 3), 1.0, 0.0
    ) + jnp.where((blk == 14) & (comp == 3), BIG_PRE, 0.0)
    sel_j = jnp.where(comp < 4, sel_j, 0.0).astype(BF)
    sel_i = jnp.where(is_pos & (comp == blk % 3) & (slot == in_p), 1.0, 0.0).astype(BF)
    sel_o = jnp.where(comp == 3, 1.0, 0.0).astype(BF)
    const_blk = iota((1, 128), 1) // 8
    const_j = jnp.where((const_blk == 12) | (const_blk == 13), 1.0, 0.0) + jnp.where(
        const_blk == 14, -BIG_PRE, 0.0
    )
    rep80 = jnp.where(iota((80, 16), 0) // 8 == iota((80, 16), 1), 1.0, 0.0).astype(BF)
    own80 = iota((80, 128), 0) % 8 == iota((80, 128), 1) % 8
    near = iota((64, 16), 1) - iota((64, 16), 0) // 8
    band64 = jnp.where((near >= 0) & (near <= 2), 1.0, 0.0).astype(BF)
    sw_half = (sw_ref[...].astype(F32) * 0.5).astype(BF)
    rw_half = (rw_ref[...].astype(F32) * 0.5).astype(BF)
    eb_half = db_ref[...] * 0.5

    def one_row(x):
        slab = wl_ref[pl.ds(pl.multiple_of(x * 80, 16), 80), :]
        geom = geom_ref[x]
        rep = jnp.where(own80, mm(rep80, geom), 0.0).astype(BF)
        gj = mm(rep, sel_j) + const_j
        occ = mm(rep, sel_o)
        s = mm(slab, sw_half) + (occ * BIG_H - BIG_H)
        return slab, geom, gj, occ, s

    @pl.loop(0, NH)
    def _(x):
        parts = [one_row(x), one_row(x + 16)]
        gj_ref[x] = jnp.concatenate([v[2].reshape(10, 8, 128) for v in parts], axis=1)
        s_ref[x] = jnp.concatenate([v[4].reshape(10, 8, 128) for v in parts], axis=1).astype(BF)

    @pl.loop(0, 32)
    def _(x):
        slab, geom, _, occ, _ = one_row(x + 1)
        at = pl.ds(pl.multiple_of(x * 64, 64), 64)
        r_ref[at, :] = mm(slab, rw_half)[8:72] + eb_half
        rel_ref[at, :] = slab.astype(F32)[8:72]
        occ_ref[at, :] = occ[8:72]
        gi_ref[x] = mm(geom, sel_i)
        near_occ = geom_ref[x].astype(F32) + geom.astype(F32) + geom_ref[x + 2].astype(F32)
        cnt_ref[at, :] = mm(mm(band64, near_occ.astype(BF)).astype(BF), sel_o) - 1.0

    lane16 = iota((16, 128), 1)
    row16 = iota((16, 128), 0)
    squared = (lane16 // 8 >= 6) & (lane16 // 8 < 12)
    linear_c = jnp.where(lane16 // 8 < 12, lane16 // 8 % 3, 3)
    eye = jnp.where((lane16 // 8 == 15) & (lane16 % 8 == row16 % 8), -BIG_PRE, 0.0)
    red_row = iota((16 * GROUP, 128 * GROUP), 0)
    red_col = iota((16 * GROUP, 128 * GROUP), 1)
    red = jnp.where(
        (red_row // (8 * GROUP) == red_col // 8 % 2)
        & (red_row // 8 % GROUP == red_col // 128)
        & (red_row % 8 == red_col // 16 % 8),
        1.0,
        0.0,
    ).astype(BF)

    def natural(x, y):
        return (x * 8 + y) * 8

    def forward(i):
        x = i // (8 // GROUP)
        y0 = i % (8 // GROUP) * GROUP
        feats = []
        for c in range(GROUP):
            y = y0 + c
            gi = jnp.concatenate(
                [
                    jnp.broadcast_to(gi_ref[x, pl.ds(y + 1, 1), :], (8, 128)),
                    jnp.broadcast_to(gi_ref[x + 16, pl.ds(y + 1, 1), :], (8, 128)),
                ],
                axis=0,
            )
            for n in range(9):
                dx, dy = step_of(n)
                reach = gj_ref[x + dx, y + dy] - gi
                if dx != 1 or dy != 1:
                    shift = jnp.where(
                        linear_c == 0, F32(dx - 1), jnp.where(linear_c == 1, F32(dy - 1), 0.0)
                    )
                    reach = reach + shift
                value = jnp.where(squared, reach * reach, reach)
                if n == 4:
                    value = value + eye
                feats.append(value.astype(BF))
        feats = jnp.concatenate(feats, axis=0)
        enc_parts = {}
        hid_parts = {}
        slope_parts = {}
        for pp in range(4):
            pre = mm(feats, w1_ref[:, pp * 256 : (pp + 1) * 256])
            enc = jnp.maximum(pre.astype(BF), BF(0))
            hh = mm(enc, bd_ref[...]).astype(BF)
            for half in range(2):
                p = 2 * pp + half
                cols = slice(half * 128, half * 128 + 128)
                own = jnp.where(row16 % 8 == p, -BIG_H, 0.0).astype(BF)
                for c in range(GROUP):
                    y = y0 + c
                    base = natural(x, y) + p
                    r = jnp.concatenate(
                        [
                            jnp.broadcast_to(r_ref[pl.ds(base, 1), :], (8, 128)),
                            jnp.broadcast_to(r_ref[pl.ds(base + 1024, 1), :], (8, 128)),
                        ],
                        axis=0,
                    ).astype(BF)
                    silus, slopes = [], []
                    for n in range(9):
                        dx, dy = step_of(n)
                        at = c * 144 + n * 16
                        h = hh[at : at + 16, cols] + (s_ref[x + dx, y + dy] + r)
                        if n == 4:
                            h = h + own
                        t = jnp.tanh(h)
                        q = BF(1) + t
                        silu = h * q
                        slope = q + silu * (BF(1) - t)
                        g_ref[x * 8 + y, p, n] = slope
                        silus.append(silu)
                        slopes.append(slope)
                    enc_parts[c, p] = tree(
                        [enc[c * 144 + n * 16 : c * 144 + n * 16 + 16, cols] for n in range(9)]
                    )
                    hid_parts[c, p] = tree(silus)
                    slope_parts[c, p] = tree(slopes)
        order = [(c, p) for c in range(GROUP) for p in range(8)]
        for parts, out in ((enc_parts, se_ref), (hid_parts, sh_ref), (slope_parts, sg_ref)):
            total = mm(red, jnp.concatenate([parts[k] for k in order], axis=0))
            base = pl.multiple_of(natural(x, y0), 8 * GROUP)
            out[pl.ds(base, 8 * GROUP), :] = total[: 8 * GROUP]
            out[pl.ds(base + 1024, 8 * GROUP), :] = total[8 * GROUP :]

    @pl.loop(0, 128 // GROUP)
    def _(i):
        forward(i)

    CH = 512

    @pl.loop(0, 2048 // CH)
    def _(k):
        at = pl.ds(pl.multiple_of(k * CH, CH), CH)
        sh = sh_ref[at, :]
        sh_b = sh.astype(BF)
        sh_l = (sh - sh_b.astype(F32)).astype(BF)
        mw = mw_ref[...]
        summed = se_ref[at, :] + mm(sh_b, mw) + mm(sh_l, mw) + cnt_ref[at, :] * mb_ref[...]
        rel = rel_ref[at, :]
        inner = mm(rel.astype(BF), nw_ref[...]) + mm(summed.astype(BF), uw_ref[...]) + nb_ref[...]
        h = inner * 0.5
        t = jnp.tanh(h)
        q = 1.0 + t
        silu = h * q
        dsilu = 0.5 * (q + silu * (1.0 - t))
        output = mm(silu.astype(BF), ow_ref[...]) + ob_ref[...]
        centred = output - jnp.mean(output, axis=-1, keepdims=True)
        inv = lax.rsqrt(jnp.mean(centred * centred, axis=-1, keepdims=True) + ln_eps)
        normed = centred * inv
        occ = occ_ref[at, :]
        gain = gain_ref[...]
        upd_ref[at, :] = (rel + occ * normed * gain).astype(BF)
        cot = cot_ref[at, :].astype(F32)
        gn = occ * cot * gain
        go = (
            (
                gn
                - jnp.mean(gn, axis=-1, keepdims=True)
                - normed * jnp.mean(gn * normed, axis=-1, keepdims=True)
            )
            * inv
        ).astype(BF)
        ginner = (mmt(go, ow_ref[...]) * dsilu).astype(BF)
        gsum = mmt(ginner, uw_ref[...]).astype(BF)
        pull = mmt(gsum, mw) * 0.5
        pull_ref[at, :] = pull
        rgrad = (pull * sg_ref[at, :]).astype(BF)
        grad_ref[at, :] = cot + mmt(ginner, nw_ref[...]) + mmt(rgrad, rw_ref[...])

    acc_ref[...] = jnp.zeros(acc_ref.shape, F32)

    @pl.loop(0, 128)
    def _(i):
        x = i // 8
        y = i % 8
        pulls = []
        for p in range(8):
            base = natural(x, y) + p
            pulls.append(
                jnp.concatenate(
                    [
                        jnp.broadcast_to(pull_ref[pl.ds(base, 1), :], (8, 128)),
                        jnp.broadcast_to(pull_ref[pl.ds(base + 1024, 1), :], (8, 128)),
                    ],
                    axis=0,
                ).astype(BF)
            )
        for n in range(9):
            dx, dy = step_of(n)
            total = tree([g_ref[i, p, n] * pulls[p] for p in range(8)])
            acc_ref[x + dx, y + dy] += total.astype(F32)

    for x in range(34):
        if x < 16:
            send_ref[x] = acc_ref[x, :, 0:8]
        elif x < 18:
            send_ref[x] = acc_ref[x, :, 0:8] + acc_ref[x - 16, :, 8:16]
        else:
            send_ref[x] = acc_ref[x - 16, :, 8:16]


def edge_call(wl, geom, cot, *weights):
    full = pl.BlockSpec(memory_space=pltpu.VMEM)
    return pl.pallas_call(
        edge_kernel,
        out_shape=(
            jax.ShapeDtypeStruct((2048, 128), BF),
            jax.ShapeDtypeStruct((2048, 128), F32),
            jax.ShapeDtypeStruct((34, 10, 8, 128), F32),
        ),
        in_specs=[full] * (3 + len(weights)),
        out_specs=(full, full, full),
        scratch_shapes=[
            pltpu.VMEM((NH, 10, 16, 128), F32),
            pltpu.VMEM((32, 16, 128), F32),
            pltpu.VMEM((NH, 10, 16, 128), BF),
            pltpu.VMEM((2048, 128), F32),
            pltpu.VMEM((2048, 128), F32),
            pltpu.VMEM((2048, 128), F32),
            pltpu.VMEM((2048, 128), F32),
            pltpu.VMEM((128, 1024), BF),
            pltpu.VMEM((256, 256), BF),
            pltpu.VMEM((2048, 128), F32),
            pltpu.VMEM((2048, 128), F32),
            pltpu.VMEM((2048, 128), F32),
            pltpu.VMEM((2048, 128), F32),
            pltpu.VMEM((NH, 10, 16, 128), F32),
            pltpu.VMEM((128, 8, 9, 16, 128), BF),
        ],
        compiler_params=pltpu.CompilerParams(vmem_limit_bytes=62 * 1024 * 1024),
        name="edges",
    )(wl, geom, cot, *weights)


def shifted(array, axis, by):
    size = lax.axis_size(axis)
    return lax.ppermute(array, axis, [(i, (i + by) % size) for i in range(size)])


def extended(array, sides, width):
    for axis, dim in sides:
        size, length = (lax.axis_size(axis), array.shape[dim])
        up = [(i, (i + 1) % size) for i in range(size)]
        down = [(j, i) for i, j in up]
        last = lax.slice_in_dim(array, length - width, length, axis=dim)
        first = lax.slice_in_dim(array, 0, width, axis=dim)
        before = lax.ppermute(last, axis, up)
        after = lax.ppermute(first, axis, down)
        array = jnp.concatenate([before, array, after], axis=dim)
    return array


def on_device(
    latent, position, counts, leaving, landing, cotangent, encoder_weight, encoder_bias,
    receiver_weight, sender_weight, edge_weight, edge_bias, message_weight, message_bias,
    node_weight, summed_weight, node_bias, output_weight, output_bias, norm_gain,
):
    rows_x, width_y, slot_count, latent_width = latent.shape
    slot_total = rows_x * width_y * slot_count
    capacity = leaving.shape[3]
    flat_rows = latent.reshape(slot_total, latent_width)
    depart = leaving.reshape(9, capacity)
    arrive = landing.reshape(9, capacity)
    picked = flat_rows[jnp.clip(depart, 0, slot_total - 1)]
    picked = jnp.where((depart >= 0)[..., None], picked, jnp.zeros_like(picked))
    grouped = picked.reshape(3, 3, capacity, latent_width)
    along_x = [None, grouped[1], None]
    for step_by in (1, -1):
        along_x[step_by + 1] = shifted(grouped[step_by + 1], "gx", step_by)
    half_moved = jnp.stack(along_x, axis=0)
    along_y = [None, half_moved[:, 1], None]
    for step_by in (1, -1):
        along_y[step_by + 1] = shifted(half_moved[:, step_by + 1], "gy", step_by)
    arrived = jnp.stack(along_y, axis=1).reshape(9, capacity, latent_width)
    target_slots = jnp.where(arrive >= 0, arrive, slot_total).reshape(-1)
    relocated = flat_rows.at[target_slots].set(arrived.reshape(-1, latent_width), mode="drop")
    relocated = relocated.reshape(rows_x, width_y, slot_count, latent_width)
    occupied = (jnp.arange(slot_count)[None, None, :] < counts[:, :, None]).astype(BF)
    geometry = jnp.concatenate([position, occupied[:, :, None, :]], axis=2)
    wide_latent = extended(relocated, (("gx", 0), ("gy", 1)), 1)
    wide_geometry = extended(geometry, (("gx", 0), ("gy", 1)), 1)
    wide_geometry = jnp.pad(wide_geometry.reshape(34, 10, 32), ((0, 0), (0, 6), (0, 96)))
    line = lambda v: v.reshape(1, -1)
    updated, grad, folded = edge_call(
        wide_latent.reshape(-1, latent_width), wide_geometry,
        cotangent.reshape(slot_total, latent_width), encoder_weight, line(encoder_bias),
        receiver_weight, sender_weight, edge_weight, line(edge_bias), message_weight,
        line(message_bias), node_weight, summed_weight, line(node_bias), output_weight,
        line(output_bias), line(norm_gain),
    )
    for step_by in (1, -1):
        edge_row = folded[rows_x + 1] if step_by == 1 else folded[0]
        incoming = shifted(edge_row.astype(jnp.bfloat16), "gx", step_by).astype(edge_row.dtype)
        if step_by == 1:
            folded = folded.at[1].add(incoming)
        else:
            folded = folded.at[rows_x].add(incoming)
    middle_rows = folded[1 : rows_x + 1]
    for step_by in (1, -1):
        column = middle_rows[:, width_y + 1] if step_by == 1 else middle_rows[:, 0]
        incoming = shifted(column.astype(jnp.bfloat16), "gy", step_by).astype(column.dtype)
        if step_by == 1:
            middle_rows = middle_rows.at[:, 1].add(incoming)
        else:
            middle_rows = middle_rows.at[:, width_y].add(incoming)
    send_core = middle_rows[:, 1 : width_y + 1]
    grad = grad + lax.dot_general(
        send_core.astype(BF).reshape(slot_total, latent_width), sender_weight,
        (((1,), (1,)), ((), ())), preferred_element_type=F32,
    )
    return updated.reshape(latent.shape), grad.reshape(latent.shape)


def solution(mesh):
    split = P("gx", "gy", None, None)
    return jax.shard_map(
        on_device,
        mesh=mesh,
        in_specs=(split, split, P("gx", "gy"), split, split, split) + (P(),) * 14,
        out_specs=(split, split),
        check_vma=False,
    )
```

```python
import jax
import jax.numpy as jnp
from jax import lax
from jax.experimental import pallas as pl
from jax.experimental.pallas import tpu as pltpu
from jax.sharding import PartitionSpec as P

ln_eps = 1e-05
F32 = jnp.float32
BF = jnp.bfloat16
BIG_PRE = 4096.0
BIG_H = 131072.0
NH = 18
MESH = pl.DeviceIdType.MESH
DIRECTIONS = [k for k in range(9) if k != 4]
GROUP = 8


def mm(a, b):
    return jnp.dot(a, b, preferred_element_type=F32)


def mmt(a, b):
    return lax.dot_general(a, b, (((1,), (1,)), ((), ())), preferred_element_type=F32)


def iota(shape, dim):
    return lax.broadcasted_iota(jnp.int32, shape, dim)


def tree(parts):
    parts = list(parts)
    while len(parts) > 1:
        parts = [
            parts[i] + parts[i + 1] if i + 1 < len(parts) else parts[i]
            for i in range(0, len(parts), 2)
        ]
    return parts[0]


def step_of(n):
    return n // 3, n % 3


def neighbour(k):
    dx, dy = step_of(k)
    nx, ny = lax.axis_size("gx"), lax.axis_size("gy")
    return (
        lax.rem(lax.axis_index("gx") + (dx - 1 + nx), nx),
        lax.rem(lax.axis_index("gy") + (dy - 1 + ny), ny),
    )


def greet():
    barrier = pltpu.get_barrier_semaphore()
    for k in DIRECTIONS:
        pl.semaphore_signal(barrier, inc=1, device_id=neighbour(k), device_id_type=MESH)
    pl.semaphore_wait(barrier, 8)


def send(k, source, target, send_sem, recv_sem):
    copy = pltpu.make_async_remote_copy(
        src_ref=source, dst_ref=target, send_sem=send_sem.at[k], recv_sem=recv_sem.at[k],
        device_id=neighbour(k), device_id_type=MESH,
    )
    copy.start()
    return copy


def rim_slot(k):
    dx, dy = step_of(k)
    if dy == 1:
        return 0, dx // 2
    if dx == 1:
        return 1, dy // 2
    return 2, dx // 2 * 2 + dy // 2


def move_kernel(
    lat_ref, leave_ref, land_ref, geo_ref,
    rel_ref, hx_ref, hy_ref, hc_ref, gin_ref,
    out_buf, in_buf, sx, sy, sc, tx, ty, tc, pick_ref, place_ref, cat_ref,
    send1, recv1, send2, recv2,
):
    leave = leave_ref[...]
    upper = jnp.where(leave < 0, -64, leave // 64 * 64)
    lower = (leave - upper).astype(F32)
    upper = upper.astype(F32)
    eye = iota((64, 64), 0) == iota((64, 64), 1)
    ones = jnp.ones((64, 128), BF)
    slots = iota((64, 128), 1).astype(F32)
    for k in range(9):
        column = mm(jnp.where(eye, upper[k : k + 1], 0.0).astype(BF), ones) + mm(
            jnp.where(eye, lower[k : k + 1], 0.0).astype(BF), ones
        )
        for t in range(16):
            pick_ref[k * 64 : k * 64 + 64, t * 128 : t * 128 + 128] = jnp.where(
                column == slots + t * 128.0, 1.0, 0.0
            ).astype(BF)
    picked = mm(pick_ref[...], lat_ref[...]).astype(BF)
    edges = jnp.where(
        iota((64, 256), 1) == iota((64, 256), 0) % 32 * 8 + iota((64, 256), 0) // 32 * 7, 1.0, 0.0
    ).astype(BF)
    geo_y = mm(edges, geo_ref[...]).astype(BF)
    for k in range(9):
        dx, dy = step_of(k)
        out_buf[k, 0:64] = picked[k * 64 : k * 64 + 64]
        if dx == 1 and dy != 1:
            out_buf[k, 64:96] = geo_y[dy // 2 * 32 : dy // 2 * 32 + 32]
        else:
            first = 0 if dx == 0 else 224
            out_buf[k, 64:96] = geo_ref[first : first + 32]
    greet()
    first = [send(k, out_buf.at[k], in_buf.at[k], send1, recv1) for k in DIRECTIONS]
    land = land_ref[...]
    for t in range(5):
        if t < 4:
            row = jnp.concatenate([land[2 * t : 2 * t + 1], land[2 * t + 1 : 2 * t + 2]], axis=1)
        else:
            row = jnp.concatenate([land[8:9], jnp.full((1, 64), -1, jnp.int32)], axis=1)
        for u in range(8):
            place_ref[u * 256 : u * 256 + 256, t * 128 : t * 128 + 128] = jnp.where(
                iota((256, 128), 0) + u * 256 == row, 1.0, 0.0
            ).astype(BF)
    cat_ref[:, 128:256] = jnp.ones((640, 128), BF)
    cat_ref[576:640, 0:128] = jnp.zeros((64, 128), BF)
    cat_ref[256:320, 0:128] = picked[256:320]
    for copy in first:
        copy.wait()
    for k in DIRECTIONS:
        cat_ref[k * 64 : k * 64 + 64, 0:128] = in_buf[k, 0:64]
        gin_ref[k] = in_buf[k, 64:96]
    gin_ref[4] = jnp.zeros((32, 128), BF)
    for u in range(4):
        at = slice(u * 512, u * 512 + 512)
        placed = mm(place_ref[at, :], cat_ref[...])
        rows = lat_ref[at, :].astype(F32) * (1.0 - placed[:, 128:256]) + placed[:, 0:128]
        rel_ref[at, :] = rows.astype(BF)
        cells = rows.reshape(8, 8, 8, 128)
        sy[0, u * 64 : u * 64 + 64] = cells[:, 0].reshape(64, 128).astype(BF)
        sy[1, u * 64 : u * 64 + 64] = cells[:, 7].reshape(64, 128).astype(BF)
        if u == 0:
            sx[0] = rows[0:64].astype(BF)
            sc[0] = rows[0:16].astype(BF)
            sc[1] = rows[48:64].astype(BF)
        if u == 3:
            sx[1] = rows[448:512].astype(BF)
            sc[2] = rows[448:464].astype(BF)
            sc[3] = rows[496:512].astype(BF)
    pairs = ((sx, tx), (sy, ty), (sc, tc))
    second = []
    for k in DIRECTIONS:
        kind, place = rim_slot(k)
        source, target = pairs[kind]
        second.append(send(k, source.at[place], target.at[place], send2, recv2))
    for copy in second:
        copy.wait()
    hx_ref[...] = tx[...]
    hy_ref[...] = ty[...]
    hc_ref[...] = tc[...]


def move_call(latent, leaving, landing, geo):
    full = pl.BlockSpec(memory_space=pltpu.VMEM)
    rim = [(2, 64, 128), (2, 256, 128), (4, 16, 128)]
    return pl.pallas_call(
        move_kernel,
        out_shape=[jax.ShapeDtypeStruct(s, BF) for s in [(2048, 128)] + rim + [(9, 32, 128)]],
        in_specs=[full] * 4,
        out_specs=[full] * 5,
        scratch_shapes=[pltpu.VMEM((9, 96, 128), BF), pltpu.VMEM((9, 96, 128), BF)]
        + [pltpu.VMEM(s, BF) for s in rim + rim]
        + [
            pltpu.VMEM((576, 2048), BF),
            pltpu.VMEM((2048, 640), BF),
            pltpu.VMEM((640, 256), BF),
        ]
        + [pltpu.SemaphoreType.DMA((9,))] * 4,
        compiler_params=pltpu.CompilerParams(
            collective_id=0, has_side_effects=True, vmem_limit_bytes=24 * 1024 * 1024
        ),
        name="move",
    )(latent, leaving, landing, geo)


def return_kernel(
    grad_ref, rx_ref, ry_ref, rc_ref, sw_ref, out_ref, sx, sy, sc, tx, ty, tc, send_sem, recv_sem
):
    sx[...] = rx_ref[...]
    sy[...] = ry_ref[...]
    sc[...] = rc_ref[...]
    greet()
    pairs = ((sx, tx), (sy, ty), (sc, tc))
    copies = []
    for k in DIRECTIONS:
        kind, place = rim_slot(k)
        source, target = pairs[kind]
        copies.append(send(k, source.at[place], target.at[place], send_sem, recv_sem))
    out_ref[...] = grad_ref[...]
    for copy in copies:
        copy.wait()
    sw = sw_ref[...]
    for side in range(2):
        at = 31 if side == 0 else 0
        out_ref[at] += mmt(tx[side], sw).reshape(8, 8, 128)
        at = 7 if side == 0 else 0
        out_ref[:, at] += mmt(ty[side], sw).reshape(32, 8, 128)
    corner = mmt(tc[...].reshape(64, 128), sw).reshape(4, 16, 128)[:, 0:8]
    out_ref[31, 7] += corner[0]
    out_ref[31, 0] += corner[1]
    out_ref[0, 7] += corner[2]
    out_ref[0, 0] += corner[3]


def return_call(grad, rx, ry, rc, sender_weight):
    full = pl.BlockSpec(memory_space=pltpu.VMEM)
    rim = [(2, 64, 128), (2, 256, 128), (4, 16, 128)]
    return pl.pallas_call(
        return_kernel,
        out_shape=jax.ShapeDtypeStruct((32, 8, 8, 128), F32),
        in_specs=[full] * 5,
        out_specs=full,
        scratch_shapes=[pltpu.VMEM(s, BF) for s in rim + rim] + [pltpu.SemaphoreType.DMA((9,))] * 2,
        compiler_params=pltpu.CompilerParams(
            collective_id=1, has_side_effects=True, vmem_limit_bytes=24 * 1024 * 1024
        ),
        name="give_back",
    )(grad, rx, ry, rc, sender_weight)


def edge_kernel(
    rel_ref, hx_ref, hy_ref, hc_ref, geo_ref, gin_ref, cot_ref,
    ew_ref, eb_ref, rw_ref, sw_ref, dw_ref, db_ref, mw_ref, mb_ref,
    nw_ref, uw_ref, nb_ref, ow_ref, ob_ref, gain_ref,
    upd_ref, grad_ref, rx_ref, ry_ref, rc_ref,
    gj_ref, gi_ref, sf_ref, s_ref, r_ref, occ_ref, cc_ref, w1_ref, bd_ref,
    se_ref, sh_ref, sg_ref, pull_ref, acc_ref, g_ref,
):
    lane = iota((128, 128), 1)
    row = iota((128, 128), 0)
    whole = ew_ref[...]
    high = whole.astype(BF).astype(F32)
    low = whole - high
    bias_high = eb_ref[...].astype(BF).astype(F32)
    bias_low = eb_ref[...] - bias_high
    wide = lambda v: jnp.broadcast_to(v, (8, 128))
    blocks = [wide(high[c : c + 1]) for c in range(3)]
    blocks += [wide(low[c : c + 1]) for c in range(3)]
    blocks += [wide(high[3:4])] * 3 + [wide(low[3:4])] * 3
    blocks += [wide(bias_high), wide(bias_low)]
    blocks += [jnp.ones((16, 128), F32)]
    stacked = jnp.concatenate(blocks, axis=0)
    for p in range(8):
        w1_ref[:, p * 128 : (p + 1) * 128] = jnp.where(row % 8 == p, stacked, 0.0).astype(BF)
    half_w = (dw_ref[...].astype(F32) * 0.5).astype(BF)
    bd_ref[...] = jnp.zeros((256, 256), BF)
    bd_ref[0:128, 0:128] = half_w
    bd_ref[128:256, 128:256] = half_w

    comp = row // 8
    slot = row % 8
    blk = lane // 8
    in_p = lane % 8
    is_pos = blk < 12
    sel_j = jnp.where(
        is_pos & (comp == blk % 3), 1.0, 0.0
    ) + jnp.where((blk == 14) & (comp == 3), BIG_PRE, 0.0)
    sel_j = jnp.where(comp < 4, sel_j, 0.0).astype(BF)
    sel_i = jnp.where(is_pos & (comp == blk % 3) & (slot == in_p), 1.0, 0.0).astype(BF)
    sel_o = jnp.where(comp == 3, 1.0, 0.0).astype(BF)
    const_blk = iota((1, 128), 1) // 8
    const_j = jnp.where((const_blk == 12) | (const_blk == 13), 1.0, 0.0) + jnp.where(
        const_blk == 14, -BIG_PRE, 0.0
    )
    sw_half = (sw_ref[...].astype(F32) * 0.5).astype(BF)
    rw_half = (rw_ref[...].astype(F32) * 0.5).astype(BF)
    eb_half = db_ref[...] * 0.5

    def sender_rows(rows, cells, offset, count):
        size = cells.shape[0]
        spread = jnp.where(
            iota((count * 8, size), 0) // 8 + offset == iota((count * 8, size), 1), 1.0, 0.0
        ).astype(BF)
        every = mm(spread, cells)
        own = iota((count * 8, 128), 0) % 8 == iota((count * 8, 128), 1) % 8
        rep = jnp.where(own, every, 0.0).astype(BF)
        gj = mm(rep, sel_j) + const_j
        occ = mm(rep, sel_o)
        s = mm(rows, sw_half)[: count * 8] + (occ * BIG_H - BIG_H)
        number = mm(every.astype(BF), sel_o)
        return gj, s, number, occ

    def fill(where, values, shape):
        for table, value in zip((gj_ref, sf_ref, cc_ref), values):
            table[where] = value.reshape(shape)

    for u in range(4):
        at = slice(u * 512, u * 512 + 512)
        rows = rel_ref[at, :]
        gj, s, number, occ = sender_rows(rows, geo_ref[u * 64 : u * 64 + 64], 0, 64)
        fill((slice(1 + 8 * u, 9 + 8 * u), slice(1, 9)), (gj, s, number), (8, 8, 8, 128))
        occ_ref[at, :] = occ
        r_ref[at, :] = mm(rows, rw_half) + eb_half
        gi_ref[u * 64 : u * 64 + 64] = mm(geo_ref[u * 64 : u * 64 + 64], sel_i)
    for side in range(2):
        k = 1 if side == 0 else 7
        values = sender_rows(hx_ref[side], gin_ref[k], 0 if side == 0 else 24, 8)[:3]
        fill((33 if side == 0 else 0, slice(1, 9)), values, (8, 8, 128))
        k = 3 if side == 0 else 5
        values = sender_rows(hy_ref[side], gin_ref[k], 0, 32)[:3]
        fill((slice(1, 33), 9 if side == 0 else 0), values, (32, 8, 128))
    for place, (k, first, x, y) in enumerate(((0, 0, 33, 9), (2, 7, 33, 0), (6, 24, 0, 9), (8, 31, 0, 0))):
        rows = hc_ref[place]
        gj, s, number, _ = sender_rows(rows, gin_ref[k], first - (first % 8 != 0), 2)
        at = 8 if first % 8 else 0
        fill((x, y), (gj[at : at + 8], s[at : at + 8], number[at : at + 8]), (8, 128))

    @pl.loop(0, NH)
    def _(x):
        s_ref[x] = jnp.concatenate([sf_ref[x], sf_ref[x + 16]], axis=1).astype(BF)

    lane16 = iota((16, 128), 1)
    row16 = iota((16, 128), 0)
    squared = (lane16 // 8 >= 6) & (lane16 // 8 < 12)
    linear_c = jnp.where(lane16 // 8 < 12, lane16 // 8 % 3, 3)
    eye = jnp.where((lane16 // 8 == 15) & (lane16 % 8 == row16 % 8), -BIG_PRE, 0.0)
    red_row = iota((16 * GROUP, 128 * GROUP), 0)
    red_col = iota((16 * GROUP, 128 * GROUP), 1)
    red = jnp.where(
        (red_row // (8 * GROUP) == red_col // 8 % 2)
        & (red_row // 8 % GROUP == red_col // 128)
        & (red_row % 8 == red_col // 16 % 8),
        1.0,
        0.0,
    ).astype(BF)

    def natural(x, y):
        return (x * 8 + y) * 8

    def forward(i):
        x = i // (8 // GROUP)
        y0 = i % (8 // GROUP) * GROUP
        feats = []
        for c in range(GROUP):
            y = y0 + c
            gi = jnp.concatenate(
                [
                    jnp.broadcast_to(gi_ref[pl.ds(x * 8 + y, 1), :], (8, 128)),
                    jnp.broadcast_to(gi_ref[pl.ds(x * 8 + y + 128, 1), :], (8, 128)),
                ],
                axis=0,
            )
            for n in range(9):
                dx, dy = step_of(n)
                reach = (
                    jnp.concatenate([gj_ref[x + dx, y + dy], gj_ref[x + 16 + dx, y + dy]], axis=0)
                    - gi
                )
                if dx != 1 or dy != 1:
                    shift = jnp.where(
                        linear_c == 0, F32(dx - 1), jnp.where(linear_c == 1, F32(dy - 1), 0.0)
                    )
                    reach = reach + shift
                value = jnp.where(squared, reach * reach, reach)
                if n == 4:
                    value = value + eye
                feats.append(value.astype(BF))
        feats = jnp.concatenate(feats, axis=0)
        enc_parts = {}
        hid_parts = {}
        slope_parts = {}
        for pp in range(4):
            pre = mm(feats, w1_ref[:, pp * 256 : (pp + 1) * 256])
            enc = jnp.maximum(pre.astype(BF), BF(0))
            hh = mm(enc, bd_ref[...]).astype(BF)
            for half in range(2):
                p = 2 * pp + half
                cols = slice(half * 128, half * 128 + 128)
                own = jnp.where(row16 % 8 == p, -BIG_H, 0.0).astype(BF)
                for c in range(GROUP):
                    y = y0 + c
                    base = natural(x, y) + p
                    r = jnp.concatenate(
                        [
                            jnp.broadcast_to(r_ref[pl.ds(base, 1), :], (8, 128)),
                            jnp.broadcast_to(r_ref[pl.ds(base + 1024, 1), :], (8, 128)),
                        ],
                        axis=0,
                    ).astype(BF)
                    silus, slopes = [], []
                    for n in range(9):
                        dx, dy = step_of(n)
                        at = c * 144 + n * 16
                        h = hh[at : at + 16, cols] + (s_ref[x + dx, y + dy] + r)
                        if n == 4:
                            h = h + own
                        t = jnp.tanh(h)
                        q = BF(1) + t
                        silu = h * q
                        slope = q + silu * (BF(1) - t)
                        g_ref[x * 8 + y, p, n] = slope
                        silus.append(silu)
                        slopes.append(slope)
                    enc_parts[c, p] = tree(
                        [enc[c * 144 + n * 16 : c * 144 + n * 16 + 16, cols] for n in range(9)]
                    )
                    hid_parts[c, p] = tree(silus)
                    slope_parts[c, p] = tree(slopes)
        order = [(c, p) for c in range(GROUP) for p in range(8)]
        for parts, out in ((enc_parts, se_ref), (hid_parts, sh_ref), (slope_parts, sg_ref)):
            total = mm(red, jnp.concatenate([parts[k] for k in order], axis=0))
            base = pl.multiple_of(natural(x, y0), 8 * GROUP)
            out[pl.ds(base, 8 * GROUP), :] = total[: 8 * GROUP]
            out[pl.ds(base + 1024, 8 * GROUP), :] = total[8 * GROUP :]

    @pl.loop(0, 128 // GROUP)
    def _(i):
        forward(i)

    CH = 512

    @pl.loop(0, 2048 // CH)
    def _(k):
        wide_x = CH // 64
        near_y = cc_ref[pl.ds(k * wide_x, wide_x + 2)]
        near_y = near_y[:, 0:8] + near_y[:, 1:9] + near_y[:, 2:10]
        near = near_y[0:wide_x] + near_y[1 : wide_x + 1] + near_y[2 : wide_x + 2]
        number = near.reshape(CH, 128) - 1.0
        at = pl.ds(pl.multiple_of(k * CH, CH), CH)
        sh = sh_ref[at, :]
        sh_b = sh.astype(BF)
        sh_l = (sh - sh_b.astype(F32)).astype(BF)
        mw = mw_ref[...]
        summed = se_ref[at, :] + mm(sh_b, mw) + mm(sh_l, mw) + number * mb_ref[...]
        inner = mm(rel_ref[at, :], nw_ref[...]) + mm(summed.astype(BF), uw_ref[...]) + nb_ref[...]
        h = inner * 0.5
        t = jnp.tanh(h)
        q = 1.0 + t
        silu = h * q
        dsilu = 0.5 * (q + silu * (1.0 - t))
        output = mm(silu.astype(BF), ow_ref[...]) + ob_ref[...]
        centred = output - jnp.mean(output, axis=-1, keepdims=True)
        inv = lax.rsqrt(jnp.mean(centred * centred, axis=-1, keepdims=True) + ln_eps)
        normed = centred * inv
        occ = occ_ref[at, :]
        gain = gain_ref[...]
        upd_ref[at, :] = (rel_ref[at, :].astype(F32) + occ * normed * gain).astype(BF)
        cot = cot_ref[at, :].astype(F32)
        gn = occ * cot * gain
        go = (
            (
                gn
                - jnp.mean(gn, axis=-1, keepdims=True)
                - normed * jnp.mean(gn * normed, axis=-1, keepdims=True)
            )
            * inv
        ).astype(BF)
        ginner = (mmt(go, ow_ref[...]) * dsilu).astype(BF)
        gsum = mmt(ginner, uw_ref[...]).astype(BF)
        pull = mmt(gsum, mw) * 0.5
        pull_ref[at, :] = pull
        rgrad = (pull * sg_ref[at, :]).astype(BF)
        grad_ref[at, :] = cot + mmt(ginner, nw_ref[...]) + mmt(rgrad, rw_ref[...])

    acc_ref[...] = jnp.zeros(acc_ref.shape, F32)

    @pl.loop(0, 128)
    def _(i):
        x = i // 8
        y = i % 8
        pulls = []
        for p in range(8):
            base = natural(x, y) + p
            pulls.append(
                jnp.concatenate(
                    [
                        jnp.broadcast_to(pull_ref[pl.ds(base, 1), :], (8, 128)),
                        jnp.broadcast_to(pull_ref[pl.ds(base + 1024, 1), :], (8, 128)),
                    ],
                    axis=0,
                ).astype(BF)
            )
        for n in range(9):
            dx, dy = step_of(n)
            total = tree([g_ref[i, p, n] * pulls[p] for p in range(8)])
            acc_ref[x + dx, y + dy] += total.astype(F32)

    def sent(x):
        if x < 16:
            return acc_ref[x, :, 0:8]
        if x < 18:
            return acc_ref[x, :, 0:8] + acc_ref[x - 16, :, 8:16]
        return acc_ref[x - 16, :, 8:16]

    for u in range(4):
        rows = [sent(1 + 8 * u + j) for j in range(8)]
        core = jnp.concatenate([v[1:9].reshape(64, 128) for v in rows], axis=0).astype(BF)
        at = slice(u * 512, u * 512 + 512)
        grad_ref[at, :] += mmt(core, sw_ref[...])
        for side in range(2):
            rim = jnp.concatenate([v[9 * side] for v in rows], axis=0).astype(BF)
            ry_ref[side, u * 64 : u * 64 + 64] = rim
    for side in range(2):
        row = sent(33 * side)
        rx_ref[side] = row[1:9].reshape(64, 128).astype(BF)
        for end in range(2):
            cell = row[9 * end]
            rc_ref[2 * side + end] = jnp.concatenate([cell, jnp.zeros_like(cell)], axis=0).astype(BF)


def edge_call(*operands):
    full = pl.BlockSpec(memory_space=pltpu.VMEM)
    return pl.pallas_call(
        edge_kernel,
        out_shape=(
            jax.ShapeDtypeStruct((2048, 128), BF),
            jax.ShapeDtypeStruct((2048, 128), F32),
            jax.ShapeDtypeStruct((2, 64, 128), BF),
            jax.ShapeDtypeStruct((2, 256, 128), BF),
            jax.ShapeDtypeStruct((4, 16, 128), BF),
        ),
        in_specs=[full] * len(operands),
        out_specs=(full,) * 5,
        scratch_shapes=[
            pltpu.VMEM((34, 10, 8, 128), F32),
            pltpu.VMEM((256, 128), F32),
            pltpu.VMEM((34, 10, 8, 128), F32),
            pltpu.VMEM((NH, 10, 16, 128), BF),
            pltpu.VMEM((2048, 128), F32),
            pltpu.VMEM((2048, 128), F32),
            pltpu.VMEM((34, 10, 8, 128), F32),
            pltpu.VMEM((128, 1024), BF),
            pltpu.VMEM((256, 256), BF),
            pltpu.VMEM((2048, 128), F32),
            pltpu.VMEM((2048, 128), F32),
            pltpu.VMEM((2048, 128), F32),
            pltpu.VMEM((2048, 128), F32),
            pltpu.VMEM((NH, 10, 16, 128), F32),
            pltpu.VMEM((128, 8, 9, 16, 128), BF),
        ],
        compiler_params=pltpu.CompilerParams(vmem_limit_bytes=62 * 1024 * 1024),
        name="edges",
    )(*operands)


def on_device(
    latent, position, counts, leaving, landing, cotangent, encoder_weight, encoder_bias,
    receiver_weight, sender_weight, edge_weight, edge_bias, message_weight, message_bias,
    node_weight, summed_weight, node_bias, output_weight, output_bias, norm_gain,
):
    occupied = (jnp.arange(8)[None, :] < counts.reshape(256, 1)).astype(BF)
    geo = jnp.concatenate([position.reshape(256, 24), occupied], axis=1)
    geo = jnp.pad(geo, ((0, 0), (0, 96)))
    relocated, hx, hy, hc, gin = move_call(
        latent.reshape(2048, 128), leaving.reshape(9, 64), landing.reshape(9, 64), geo
    )
    line = lambda v: v.reshape(1, -1)
    updated, grad, rx, ry, rc = edge_call(
        relocated, hx, hy, hc, geo, gin, cotangent.reshape(2048, 128), encoder_weight,
        line(encoder_bias), receiver_weight, sender_weight, edge_weight, line(edge_bias),
        message_weight, line(message_bias), node_weight, summed_weight, line(node_bias),
        output_weight, line(output_bias), line(norm_gain),
    )
    grad = return_call(grad.reshape(latent.shape), rx, ry, rc, sender_weight)
    return updated.reshape(latent.shape), grad


def solution(mesh):
    split = P("gx", "gy", None, None)
    return jax.shard_map(
        on_device,
        mesh=mesh,
        in_specs=(split, split, P("gx", "gy"), split, split, split) + (P(),) * 14,
        out_specs=(split, split),
        check_vma=False,
    )
```

```python
import jax
import jax.numpy as jnp
from jax import lax
from jax.experimental import pallas as pl
from jax.experimental.pallas import tpu as pltpu
from jax.sharding import PartitionSpec as P

ln_eps = 1e-05
F32 = jnp.float32
BF = jnp.bfloat16
BIG_PRE = 4096.0
BIG_H = 131072.0
NH = 18
MESH = pl.DeviceIdType.MESH
DIRECTIONS = [k for k in range(9) if k != 4]


def mm(a, b):
    return jnp.dot(a, b, preferred_element_type=F32)


def mmt(a, b):
    return lax.dot_general(a, b, (((1,), (1,)), ((), ())), preferred_element_type=F32)


def iota(shape, dim):
    return lax.broadcasted_iota(jnp.int32, shape, dim)


def tree(parts):
    parts = list(parts)
    while len(parts) > 1:
        parts = [
            parts[i] + parts[i + 1] if i + 1 < len(parts) else parts[i]
            for i in range(0, len(parts), 2)
        ]
    return parts[0]


def step_of(n):
    return n // 3, n % 3


def neighbour(k):
    dx, dy = step_of(k)
    nx, ny = lax.axis_size("gx"), lax.axis_size("gy")
    return (
        lax.rem(lax.axis_index("gx") + (dx - 1 + nx), nx),
        lax.rem(lax.axis_index("gy") + (dy - 1 + ny), ny),
    )


def send(k, source, target, send_sem, recv_sem):
    copy = pltpu.make_async_remote_copy(
        src_ref=source, dst_ref=target, send_sem=send_sem.at[k], recv_sem=recv_sem.at[k],
        device_id=neighbour(k), device_id_type=MESH,
    )
    copy.start()
    return copy


def rim_slot(k):
    dx, dy = step_of(k)
    if dy == 1:
        return 0, dx // 2
    if dx == 1:
        return 1, dy // 2
    return 2, dx // 2 * 2 + dy // 2


def step_kernel(
    lat_ref, leave_ref, land_ref, geo_ref, cot_ref,
    ew_ref, eb_ref, rw_ref, sw_ref, dw_ref, db_ref, mw_ref, mb_ref,
    nw_ref, uw_ref, nb_ref, ow_ref, ob_ref, gain_ref,
    upd_ref, grad_ref,
    out_buf, in_buf, sx, sy, sc, tx, ty, tc, bx, by, bc, dx_buf, dy_buf, dc_buf,
    hot_ref, cat_ref, rel_ref,
    gj_ref, gi_ref, sf_ref, s_ref, r_ref, occ_ref, cc_ref, w1_ref, bd_ref, red_ref,
    se_ref, sh_ref, sg_ref, g_ref,
    send1, recv1, send2, recv2, send3, recv3,
):
    barrier = pltpu.get_barrier_semaphore()
    for k in DIRECTIONS:
        pl.semaphore_signal(barrier, inc=1, device_id=neighbour(k), device_id_type=MESH)
    leave = leave_ref[...]
    upper = jnp.where(leave < 0, -64, leave // 64 * 64)
    lower = (leave - upper).astype(F32)
    upper = upper.astype(F32)
    eye = iota((64, 64), 0) == iota((64, 64), 1)
    ones = jnp.ones((64, 128), BF)
    slots = iota((64, 128), 1).astype(F32)
    for k in range(9):
        column = mm(jnp.where(eye, upper[k : k + 1], 0.0).astype(BF), ones) + mm(
            jnp.where(eye, lower[k : k + 1], 0.0).astype(BF), ones
        )
        for t in range(16):
            row = t // 4 * 576 + k * 64
            hot_ref[row : row + 64, t % 4 * 128 : t % 4 * 128 + 128] = jnp.where(
                column == slots + t * 128.0, 1.0, 0.0
            ).astype(BF)
    picked = tree(
        [
            mm(hot_ref[u * 576 : u * 576 + 576, 0:512], lat_ref[u * 512 : u * 512 + 512, :])
            for u in range(4)
        ]
    ).astype(BF)
    edges = jnp.where(
        iota((64, 256), 1) == iota((64, 256), 0) % 32 * 8 + iota((64, 256), 0) // 32 * 7, 1.0, 0.0
    ).astype(BF)
    geo_y = mm(edges, geo_ref[...]).astype(BF)
    for k in range(9):
        dx, dy = step_of(k)
        out_buf[k, 0:64] = picked[k * 64 : k * 64 + 64]
        if dx == 1 and dy != 1:
            out_buf[k, 64:96] = geo_y[dy // 2 * 32 : dy // 2 * 32 + 32]
        else:
            first = 0 if dx == 0 else 224
            out_buf[k, 64:96] = geo_ref[first : first + 32]
    pl.semaphore_wait(barrier, 8)
    first = [send(k, out_buf.at[k], in_buf.at[k], send1, recv1) for k in DIRECTIONS]
    land = land_ref[...]
    for t in range(5):
        if t < 4:
            row = jnp.concatenate([land[2 * t : 2 * t + 1], land[2 * t + 1 : 2 * t + 2]], axis=1)
        else:
            row = jnp.concatenate([land[8:9], jnp.full((1, 64), -1, jnp.int32)], axis=1)
        for u in range(8):
            hot_ref[u * 256 : u * 256 + 256, t * 128 : t * 128 + 128] = jnp.where(
                iota((256, 128), 0) + u * 256 == row, 1.0, 0.0
            ).astype(BF)
    cat_ref[:, 128:256] = jnp.ones((640, 128), BF)
    cat_ref[576:640, 0:128] = jnp.zeros((64, 128), BF)
    cat_ref[256:320, 0:128] = picked[256:320]
    lane = iota((128, 128), 1)
    row = iota((128, 128), 0)
    whole = ew_ref[...]
    high = whole.astype(BF).astype(F32)
    low = whole - high
    bias_high = eb_ref[...].astype(BF).astype(F32)
    bias_low = eb_ref[...] - bias_high
    wide = lambda v: jnp.broadcast_to(v, (8, 128))
    blocks = [wide(high[c : c + 1]) for c in range(3)]
    blocks += [wide(low[c : c + 1]) for c in range(3)]
    blocks += [wide(high[3:4])] * 3 + [wide(low[3:4])] * 3
    blocks += [wide(bias_high), wide(bias_low)]
    blocks += [jnp.ones((16, 128), F32)]
    stacked = jnp.concatenate(blocks, axis=0)
    for p in range(8):
        w1_ref[:, p * 128 : (p + 1) * 128] = jnp.where(row % 8 == p, stacked, 0.0).astype(BF)
    half_w = (dw_ref[...].astype(F32) * 0.5).astype(BF)
    bd_ref[...] = jnp.zeros((256, 256), BF)
    bd_ref[0:128, 0:128] = half_w
    bd_ref[128:256, 128:256] = half_w

    comp = row // 8
    slot = row % 8
    blk = lane // 8
    in_p = lane % 8
    is_pos = blk < 12
    sel_j = jnp.where(
        is_pos & (comp == blk % 3), 1.0, 0.0
    ) + jnp.where((blk == 14) & (comp == 3), BIG_PRE, 0.0)
    sel_j = jnp.where(comp < 4, sel_j, 0.0).astype(BF)
    sel_i = jnp.where(is_pos & (comp == blk % 3) & (slot == in_p), 1.0, 0.0).astype(BF)
    sel_o = jnp.where(comp == 3, 1.0, 0.0).astype(BF)
    const_blk = iota((1, 128), 1) // 8
    const_j = jnp.where((const_blk == 12) | (const_blk == 13), 1.0, 0.0) + jnp.where(
        const_blk == 14, -BIG_PRE, 0.0
    )
    sw_half = (sw_ref[...].astype(F32) * 0.5).astype(BF)
    rw_half = (rw_ref[...].astype(F32) * 0.5).astype(BF)
    eb_half = db_ref[...] * 0.5

    red_row = iota((128, 1024), 0)
    red_col = iota((128, 1024), 1)
    red_ref[...] = jnp.where(
        (red_row // 64 == red_col // 8 % 2)
        & (red_row // 8 % 8 == red_col // 16 % 8)
        & (red_row % 8 == red_col // 128),
        1.0,
        0.0,
    ).astype(BF)

    def cell_rows(cells, offset, count):
        size = cells.shape[0]
        lift = jnp.where(
            iota((count * 8, size), 0) // 8 + offset == iota((count * 8, size), 1), 1.0, 0.0
        ).astype(BF)
        every = mm(lift, cells).astype(BF)
        own = iota((count * 8, 128), 0) % 8 == iota((count * 8, 128), 1) % 8
        rep = jnp.where(own, every.astype(F32), 0.0).astype(BF)
        occ = mm(rep, sel_o)
        return mm(rep, sel_j) + const_j, occ * BIG_H - BIG_H, mm(every, sel_o), occ, every

    def fill(where, values, shape):
        for table, value in zip((gj_ref, sf_ref, cc_ref), values):
            table[where] = value.reshape(shape)

    for u in range(4):
        at = slice(u * 512, u * 512 + 512)
        gj, mask, number, occ, every = cell_rows(geo_ref[u * 64 : u * 64 + 64], 0, 64)
        cells = slice(8 * u, 8 * u + 8)
        fill((slice(1 + 8 * u, 9 + 8 * u), slice(1, 9)), (gj, mask, number), (8, 8, 8, 128))
        occ_ref[at, :] = occ
        gi_ref[cells] = mm(every, sel_i).reshape(8, 8, 8, 128)
    for copy in first:
        copy.wait()
    for k in DIRECTIONS:
        cat_ref[k * 64 : k * 64 + 64, 0:128] = in_buf[k, 0:64]
    for u in range(4):
        at = slice(u * 512, u * 512 + 512)
        placed = mm(hot_ref[at, :], cat_ref[...])
        rows = lat_ref[at, :].astype(F32) * (1.0 - placed[:, 128:256]) + placed[:, 0:128]
        rel_ref[at, :] = rows.astype(BF)
        cells = rows.reshape(8, 8, 8, 128)
        sy[0, u * 64 : u * 64 + 64] = cells[:, 0].reshape(64, 128).astype(BF)
        sy[1, u * 64 : u * 64 + 64] = cells[:, 7].reshape(64, 128).astype(BF)
        if u == 0:
            sx[0] = rows[0:64].astype(BF)
            sc[0] = rows[0:16].astype(BF)
            sc[1] = rows[48:64].astype(BF)
        if u == 3:
            sx[1] = rows[448:512].astype(BF)
            sc[2] = rows[448:464].astype(BF)
            sc[3] = rows[496:512].astype(BF)
    pairs = ((sx, tx), (sy, ty), (sc, tc))
    second = []
    for k in DIRECTIONS:
        kind, place = rim_slot(k)
        source, target = pairs[kind]
        second.append(send(k, source.at[place], target.at[place], send2, recv2))
    for side in range(2):
        k = 1 if side == 0 else 7
        values = cell_rows(in_buf[k, 64:96], 0 if side == 0 else 24, 8)[:3]
        fill((33 if side == 0 else 0, slice(1, 9)), values, (8, 8, 128))
        k = 3 if side == 0 else 5
        values = cell_rows(in_buf[k, 64:96], 0, 32)[:3]
        fill((slice(1, 33), 9 if side == 0 else 0), values, (32, 8, 128))
    corners = ((0, 0, 33, 9), (2, 7, 33, 0), (6, 24, 0, 9), (8, 31, 0, 0))
    for k, first_row, x, y in corners:
        odd = first_row % 8 != 0
        values = cell_rows(in_buf[k, 64:96], first_row - odd, 2)[:3]
        at = 8 if odd else 0
        fill((x, y), [v[at : at + 8] for v in values], (8, 128))
    for u in range(4):
        rows = rel_ref[u * 512 : u * 512 + 512, :]
        cells = slice(8 * u, 8 * u + 8)
        sf_ref[1 + 8 * u : 9 + 8 * u, 1:9] += mm(rows, sw_half).reshape(8, 8, 8, 128)
        r_ref[cells] = (mm(rows, rw_half) + eb_half).reshape(8, 8, 8, 128)
    for copy in second:
        copy.wait()
    for side in range(2):
        x = 33 if side == 0 else 0
        sf_ref[x, 1:9] += mm(tx[side], sw_half).reshape(8, 8, 128)
        y = 9 if side == 0 else 0
        sf_ref[1:33, y] += mm(ty[side], sw_half).reshape(32, 8, 128)
    for place, (k, first_row, x, y) in enumerate(corners):
        at = 8 if first_row % 8 else 0
        sf_ref[x, y] += mm(tc[place], sw_half)[at : at + 8]

    @pl.loop(0, NH)
    def _(x):
        s_ref[x] = jnp.concatenate([sf_ref[x], sf_ref[x + 16]], axis=1).astype(BF)

    tile = (8, 16, 128)
    blk16 = iota(tile, 2) // 8
    squared = (blk16 >= 6) & (blk16 < 12)
    linear_c = jnp.where(blk16 < 12, blk16 % 3, 3)
    eye = jnp.where((blk16 == 15) & (iota(tile, 2) % 8 == iota(tile, 1) % 8), -BIG_PRE, 0.0)
    def both(ref, x):
        return jnp.concatenate([ref[x], ref[x + 16]], axis=1)

    def spread(rows, p):
        return jnp.concatenate(
            [jnp.broadcast_to(v[:, p : p + 1], (8, 8, 128)) for v in rows], axis=1
        ).reshape(128, 128)

    @pl.loop(0, 16)
    def _(x):
        gi = both(gi_ref, x)
        feats = []
        for n in range(9):
            dx, dy = step_of(n)
            reach = (
                jnp.concatenate(
                    [gj_ref[x + dx, dy : dy + 8], gj_ref[x + 16 + dx, dy : dy + 8]], axis=1
                )
                - gi
            )
            if n != 4:
                reach = reach + jnp.where(
                    linear_c == 0, float(dx - 1), jnp.where(linear_c == 1, float(dy - 1), 0.0)
                )
            value = jnp.where(squared, reach * reach, reach)
            if n == 4:
                value = value + eye
            feats.append(value.reshape(128, 128).astype(BF))
        feats = jnp.concatenate(feats, axis=0)
        own_rows = (r_ref[x], r_ref[x + 16])
        parts = [[], [], []]
        for pp in range(4):
            pre = mm(feats, w1_ref[:, pp * 256 : (pp + 1) * 256])
            enc = jnp.maximum(pre.astype(BF), BF(0))
            hh = mm(enc, bd_ref[...]).astype(BF)
            for half in range(2):
                p = 2 * pp + half
                cols = slice(half * 128, half * 128 + 128)
                r = spread(own_rows, p).astype(BF)
                pieces = [[], [], []]
                for y in range(0, 8, 2):
                    stacks = [[], [], []]
                    inside = slice(y * 16, (y + 2) * 16)
                    for n in range(9):
                        dx, dy = step_of(n)
                        at = slice(n * 128 + y * 16, n * 128 + (y + 2) * 16)
                        near = s_ref[x + dx, dy + y : dy + y + 2].reshape(32, 128)
                        h = hh[at, cols] + (near + r[inside])
                        if n == 4:
                            own = iota((32, 128), 0) % 8 == p
                            h = h + jnp.where(own, -BIG_H, 0.0).astype(BF)
                        t = jnp.tanh(h)
                        q = BF(1) + t
                        silu = h * q
                        slope = q + silu * (BF(1) - t)
                        g_ref[x, p, n, inside] = slope
                        for stack, value in zip(stacks, (enc[at, cols], silu, slope)):
                            stack.append((1, value))
                            while len(stack) > 1 and (stack[-1][0] == stack[-2][0] or n == 8):
                                last, before = stack.pop(), stack.pop()
                                stack.append((last[0] + before[0], last[1] + before[1]))
                    for piece, stack in zip(pieces, stacks):
                        piece.append(stack[0][1])
                for part, piece in zip(parts, pieces):
                    part.append(jnp.concatenate(piece, axis=0))
        for part, out in zip(parts, (se_ref, sh_ref, sg_ref)):
            total = mm(red_ref[...], jnp.concatenate(part, axis=0))
            at = pl.multiple_of(x * 64, 64)
            out[pl.ds(at, 64), :] = total[:64]
            out[pl.ds(at + 1024, 64), :] = total[64:]

    CH = 512

    @pl.loop(0, 2048 // CH)
    def _(k):
        wide_x = CH // 64
        near_y = cc_ref[pl.ds(k * wide_x, wide_x + 2)]
        near_y = near_y[:, 0:8] + near_y[:, 1:9] + near_y[:, 2:10]
        near = near_y[0:wide_x] + near_y[1 : wide_x + 1] + near_y[2 : wide_x + 2]
        number = near.reshape(CH, 128) - 1.0
        at = pl.ds(pl.multiple_of(k * CH, CH), CH)
        sh = sh_ref[at, :]
        sh_b = sh.astype(BF)
        sh_l = (sh - sh_b.astype(F32)).astype(BF)
        mw = mw_ref[...]
        summed = se_ref[at, :] + mm(sh_b, mw) + mm(sh_l, mw) + number * mb_ref[...]
        inner = mm(rel_ref[at, :], nw_ref[...]) + mm(summed.astype(BF), uw_ref[...]) + nb_ref[...]
        h = inner * 0.5
        t = jnp.tanh(h)
        q = 1.0 + t
        silu = h * q
        dsilu = 0.5 * (q + silu * (1.0 - t))
        output = mm(silu.astype(BF), ow_ref[...]) + ob_ref[...]
        centred = output - jnp.mean(output, axis=-1, keepdims=True)
        inv = lax.rsqrt(jnp.mean(centred * centred, axis=-1, keepdims=True) + ln_eps)
        normed = centred * inv
        occ = occ_ref[at, :]
        gain = gain_ref[...]
        upd_ref[at, :] = (rel_ref[at, :].astype(F32) + occ * normed * gain).astype(BF)
        cot = cot_ref[at, :].astype(F32)
        gn = occ * cot * gain
        go = (
            (
                gn
                - jnp.mean(gn, axis=-1, keepdims=True)
                - normed * jnp.mean(gn * normed, axis=-1, keepdims=True)
            )
            * inv
        ).astype(BF)
        ginner = (mmt(go, ow_ref[...]) * dsilu).astype(BF)
        gsum = mmt(ginner, uw_ref[...]).astype(BF)
        pull = mmt(gsum, mw) * 0.5
        r_ref[pl.ds(k * wide_x, wide_x)] = pull.reshape(wide_x, 8, 8, 128)
        rgrad = (pull * sg_ref[at, :]).astype(BF)
        total = cot + mmt(ginner, nw_ref[...]) + mmt(rgrad, rw_ref[...])
        grad_ref[pl.ds(k * wide_x, wide_x)] = total.reshape(wide_x, 8, 8, 128)


    sf_ref[...] = jnp.zeros(sf_ref.shape, F32)

    def tiles(x, y):
        rows = (r_ref[x, y], r_ref[x + 16, y])
        return [
            jnp.concatenate(
                [jnp.broadcast_to(v[p : p + 1], (8, 128)) for v in rows], axis=0
            )
            for p in range(8)
        ]

    @pl.loop(0, 16)
    def _(x):
        for y in range(8):
            pulls = [v.astype(BF) for v in tiles(x, y)]
            for n in range(9):
                dx, dy = step_of(n)
                total = tree([g_ref[x, p, n, y * 16 : y * 16 + 16] * pulls[p] for p in range(8)])
                total = total.astype(F32)
                sf_ref[x + dx, y + dy] += total[0:8]
                sf_ref[x + 16 + dx, y + dy] += total[8:16]

    for u in range(4):
        for side in range(2):
            edge = sf_ref[1 + 8 * u : 9 + 8 * u, 9 * side].reshape(64, 128)
            by[side, u * 64 : u * 64 + 64] = edge.astype(BF)
    for side in range(2):
        x = 33 * side
        bx[side] = sf_ref[x, 1:9].reshape(64, 128).astype(BF)
        for end in range(2):
            cell = sf_ref[x, 9 * end]
            bc[2 * side + end] = jnp.concatenate([cell, jnp.zeros_like(cell)], axis=0).astype(BF)
    pairs = ((bx, dx_buf), (by, dy_buf), (bc, dc_buf))
    third = []
    for k in DIRECTIONS:
        kind, place = rim_slot(k)
        source, target = pairs[kind]
        third.append(send(k, source.at[place], target.at[place], send3, recv3))
    sw = sw_ref[...]
    for u in range(4):
        core = sf_ref[1 + 8 * u : 9 + 8 * u, 1:9].reshape(512, 128).astype(BF)
        grad_ref[8 * u : 8 * u + 8] += mmt(core, sw).reshape(8, 8, 8, 128)
    for copy in third:
        copy.wait()
    for side in range(2):
        at = 31 if side == 0 else 0
        grad_ref[at] += mmt(dx_buf[side], sw).reshape(8, 8, 128)
        at = 7 if side == 0 else 0
        grad_ref[:, at] += mmt(dy_buf[side], sw).reshape(32, 8, 128)
    corner = mmt(dc_buf[...].reshape(64, 128), sw).reshape(4, 16, 128)[:, 0:8]
    grad_ref[31, 7] += corner[0]
    grad_ref[31, 0] += corner[1]
    grad_ref[0, 7] += corner[2]
    grad_ref[0, 0] += corner[3]


def step_call(*operands):
    full = pl.BlockSpec(memory_space=pltpu.VMEM)
    rim = [(2, 64, 128), (2, 256, 128), (4, 16, 128)]
    return pl.pallas_call(
        step_kernel,
        out_shape=(
            jax.ShapeDtypeStruct((2048, 128), BF),
            jax.ShapeDtypeStruct((32, 8, 8, 128), F32),
        ),
        in_specs=[full] * len(operands),
        out_specs=(full,) * 2,
        scratch_shapes=[pltpu.VMEM((9, 96, 128), BF), pltpu.VMEM((9, 96, 128), BF)]
        + [pltpu.VMEM(v, BF) for v in rim * 4]
        + [
            pltpu.VMEM((2304, 640), BF),
            pltpu.VMEM((640, 256), BF),
            pltpu.VMEM((2048, 128), BF),
            pltpu.VMEM((34, 10, 8, 128), F32),
            pltpu.VMEM((32, 8, 8, 128), F32),
            pltpu.VMEM((34, 10, 8, 128), F32),
            pltpu.VMEM((NH, 10, 16, 128), BF),
            pltpu.VMEM((32, 8, 8, 128), F32),
            pltpu.VMEM((2048, 128), F32),
            pltpu.VMEM((34, 10, 8, 128), F32),
            pltpu.VMEM((128, 1024), BF),
            pltpu.VMEM((256, 256), BF),
            pltpu.VMEM((128, 1024), BF),
            pltpu.VMEM((2048, 128), F32),
            pltpu.VMEM((2048, 128), F32),
            pltpu.VMEM((2048, 128), F32),
            pltpu.VMEM((16, 8, 9, 128, 128), BF),
        ]
        + [pltpu.SemaphoreType.DMA((9,))] * 6,
        compiler_params=pltpu.CompilerParams(
            collective_id=0, has_side_effects=True, vmem_limit_bytes=62 * 1024 * 1024
        ),
        name="step",
    )(*operands)


def on_device(
    latent, position, counts, leaving, landing, cotangent, encoder_weight, encoder_bias,
    receiver_weight, sender_weight, edge_weight, edge_bias, message_weight, message_bias,
    node_weight, summed_weight, node_bias, output_weight, output_bias, norm_gain,
):
    occupied = (jnp.arange(8)[None, :] < counts.reshape(256, 1)).astype(BF)
    geo = jnp.concatenate([position.reshape(256, 24), occupied], axis=1)
    geo = jnp.pad(geo, ((0, 0), (0, 96)))
    line = lambda v: v.reshape(1, -1)
    updated, grad = step_call(
        latent.reshape(2048, 128), leaving.reshape(9, 64), landing.reshape(9, 64), geo,
        cotangent.reshape(2048, 128), encoder_weight, line(encoder_bias), receiver_weight,
        sender_weight, edge_weight, line(edge_bias), message_weight, line(message_bias),
        node_weight, summed_weight, line(node_bias), output_weight, line(output_bias),
        line(norm_gain),
    )
    return updated.reshape(latent.shape), grad


def solution(mesh):
    split = P("gx", "gy", None, None)
    return jax.shard_map(
        on_device,
        mesh=mesh,
        in_specs=(split, split, P("gx", "gy"), split, split, split) + (P(),) * 14,
        out_specs=(split, split),
        check_vma=False,
    )
```

```python
import jax
import jax.numpy as jnp
from jax import lax
from jax.experimental import pallas as pl
from jax.experimental.pallas import tpu as pltpu
from jax.sharding import PartitionSpec as P

ln_eps = 1e-05
F32 = jnp.float32
BF = jnp.bfloat16
BIG_PRE = 4096.0
BIG_H = 131072.0
NH = 18
MESH = pl.DeviceIdType.MESH
DIRECTIONS = [k for k in range(9) if k != 4]


def mm(a, b):
    return jnp.dot(a, b, preferred_element_type=F32)


def mmt(a, b):
    return lax.dot_general(a, b, (((1,), (1,)), ((), ())), preferred_element_type=F32)


def iota(shape, dim):
    return lax.broadcasted_iota(jnp.int32, shape, dim)


def tree(parts):
    parts = list(parts)
    while len(parts) > 1:
        parts = [
            parts[i] + parts[i + 1] if i + 1 < len(parts) else parts[i]
            for i in range(0, len(parts), 2)
        ]
    return parts[0]


def step_of(n):
    return n // 3, n % 3


def neighbour(k):
    dx, dy = step_of(k)
    nx, ny = lax.axis_size("gx"), lax.axis_size("gy")
    return (
        lax.rem(lax.axis_index("gx") + (dx - 1 + nx), nx),
        lax.rem(lax.axis_index("gy") + (dy - 1 + ny), ny),
    )


def send(k, source, target, send_sem, recv_sem):
    copy = pltpu.make_async_remote_copy(
        src_ref=source, dst_ref=target, send_sem=send_sem.at[k], recv_sem=recv_sem.at[k],
        device_id=neighbour(k), device_id_type=MESH,
    )
    copy.start()
    return copy


def rim_slot(k):
    dx, dy = step_of(k)
    if dy == 1:
        return 0, dx // 2
    if dx == 1:
        return 1, dy // 2
    return 2, dx // 2 * 2 + dy // 2


def step_kernel(
    lat_ref, leave_ref, land_ref, place_ref, count_ref, cot_ref,
    ew_ref, eb_ref, rw_ref, sw_ref, dw_ref, db_ref, mw_ref, mb_ref,
    nw_ref, uw_ref, nb_ref, ow_ref, ob_ref, gain_ref,
    upd_ref, grad_ref,
    out_buf, in_buf, sx, sy, sc, tx, ty, tc, bx, by, bc, dx_buf, dy_buf, dc_buf,
    hot_ref, cat_ref, rel_ref, geo_ref,
    gj_ref, gi_ref, sf_ref, s_ref, r_ref, occ_ref, cc_ref, w1_ref, bd_ref, red_ref,
    se_ref, sh_ref, sg_ref, g_ref,
    send1, recv1, send2, recv2, send3, recv3,
):
    barrier = pltpu.get_barrier_semaphore()
    for k in DIRECTIONS:
        pl.semaphore_signal(barrier, inc=1, device_id=neighbour(k), device_id_type=MESH)
    unit = jnp.where(iota((32, 32), 0) == iota((32, 32), 1), 1.0, 0.0).astype(BF)
    count = count_ref[...].astype(F32)
    turned = []
    for y in range(8):
        held = jnp.where(iota((8, 32), 0).astype(F32) < count[y : y + 1], 1.0, 0.0)
        lanes_x = jnp.concatenate([place_ref[y].astype(F32), held], axis=0).astype(BF)
        turned.append(mmt(unit, lanes_x))
    turned = jnp.concatenate(turned, axis=0).astype(BF)
    cell_row = iota((256, 256), 0)
    order = jnp.where(iota((256, 256), 1) == cell_row % 8 * 32 + cell_row // 8, 1.0, 0.0).astype(BF)
    widen = jnp.where(iota((32, 128), 0) == iota((32, 128), 1), 1.0, 0.0).astype(BF)
    geo_ref[...] = mm(mm(order, turned).astype(BF), widen).astype(BF)
    leave = jnp.concatenate([leave_ref[0, k] for k in range(9)], axis=0)
    upper = jnp.where(leave < 0, -64, leave // 64 * 64)
    lower = (leave - upper).astype(F32)
    upper = upper.astype(F32)
    eye = iota((64, 64), 0) == iota((64, 64), 1)
    ones = jnp.ones((64, 128), BF)
    slots = iota((64, 128), 1).astype(F32)
    for k in range(9):
        column = mm(jnp.where(eye, upper[k : k + 1], 0.0).astype(BF), ones) + mm(
            jnp.where(eye, lower[k : k + 1], 0.0).astype(BF), ones
        )
        for t in range(16):
            row = t // 4 * 576 + k * 64
            hot_ref[row : row + 64, t % 4 * 128 : t % 4 * 128 + 128] = jnp.where(
                column == slots + t * 128.0, 1.0, 0.0
            ).astype(BF)
    picked = tree(
        [
            mm(hot_ref[u * 576 : u * 576 + 576, 0:512], lat_ref[u * 512 : u * 512 + 512, :])
            for u in range(4)
        ]
    ).astype(BF)
    edges = jnp.where(
        iota((64, 256), 1) == iota((64, 256), 0) % 32 * 8 + iota((64, 256), 0) // 32 * 7, 1.0, 0.0
    ).astype(BF)
    geo_y = mm(edges, geo_ref[...]).astype(BF)
    for k in range(9):
        dx, dy = step_of(k)
        out_buf[k, 0:64] = picked[k * 64 : k * 64 + 64]
        if dx == 1 and dy != 1:
            out_buf[k, 64:96] = geo_y[dy // 2 * 32 : dy // 2 * 32 + 32]
        else:
            first = 0 if dx == 0 else 224
            out_buf[k, 64:96] = geo_ref[first : first + 32]
    pl.semaphore_wait(barrier, 8)
    first = [send(k, out_buf.at[k], in_buf.at[k], send1, recv1) for k in DIRECTIONS]
    land = [land_ref[0, k] for k in range(9)]
    for t in range(5):
        if t < 4:
            row = jnp.concatenate([land[2 * t], land[2 * t + 1]], axis=1)
        else:
            row = jnp.concatenate([land[8], jnp.full((1, 64), -1, jnp.int32)], axis=1)
        for u in range(8):
            hot_ref[u * 256 : u * 256 + 256, t * 128 : t * 128 + 128] = jnp.where(
                iota((256, 128), 0) + u * 256 == row, 1.0, 0.0
            ).astype(BF)
    cat_ref[:, 128:256] = jnp.ones((640, 128), BF)
    cat_ref[576:640, 0:128] = jnp.zeros((64, 128), BF)
    cat_ref[256:320, 0:128] = picked[256:320]
    lane = iota((128, 128), 1)
    row = iota((128, 128), 0)
    whole = ew_ref[...]
    high = whole.astype(BF).astype(F32)
    low = whole - high
    bias_high = eb_ref[...].astype(BF).astype(F32)
    bias_low = eb_ref[...] - bias_high
    wide = lambda v: jnp.broadcast_to(v, (8, 128))
    blocks = [wide(high[c : c + 1]) for c in range(3)]
    blocks += [wide(low[c : c + 1]) for c in range(3)]
    blocks += [wide(high[3:4])] * 3 + [wide(low[3:4])] * 3
    blocks += [wide(bias_high), wide(bias_low)]
    blocks += [jnp.ones((16, 128), F32)]
    stacked = jnp.concatenate(blocks, axis=0)
    for p in range(8):
        w1_ref[:, p * 128 : (p + 1) * 128] = jnp.where(row % 8 == p, stacked, 0.0).astype(BF)
    half_w = (dw_ref[...].astype(F32) * 0.5).astype(BF)
    bd_ref[...] = jnp.zeros((256, 256), BF)
    bd_ref[0:128, 0:128] = half_w
    bd_ref[128:256, 128:256] = half_w

    comp = row // 8
    slot = row % 8
    blk = lane // 8
    in_p = lane % 8
    is_pos = blk < 12
    sel_j = jnp.where(
        is_pos & (comp == blk % 3), 1.0, 0.0
    ) + jnp.where((blk == 14) & (comp == 3), BIG_PRE, 0.0)
    sel_j = jnp.where(comp < 4, sel_j, 0.0).astype(BF)
    sel_i = jnp.where(is_pos & (comp == blk % 3) & (slot == in_p), 1.0, 0.0).astype(BF)
    sel_o = jnp.where(comp == 3, 1.0, 0.0).astype(BF)
    const_blk = iota((1, 128), 1) // 8
    const_j = jnp.where((const_blk == 12) | (const_blk == 13), 1.0, 0.0) + jnp.where(
        const_blk == 14, -BIG_PRE, 0.0
    )
    sw_half = (sw_ref[...].astype(F32) * 0.5).astype(BF)
    rw_half = (rw_ref[...].astype(F32) * 0.5).astype(BF)
    eb_half = db_ref[...] * 0.5

    red_row = iota((128, 1024), 0)
    red_col = iota((128, 1024), 1)
    red_ref[...] = jnp.where(
        (red_row // 64 == red_col // 8 % 2)
        & (red_row // 8 % 8 == red_col // 16 % 8)
        & (red_row % 8 == red_col // 128),
        1.0,
        0.0,
    ).astype(BF)

    def cell_rows(cells, offset, count):
        size = cells.shape[0]
        lift = jnp.where(
            iota((count * 8, size), 0) // 8 + offset == iota((count * 8, size), 1), 1.0, 0.0
        ).astype(BF)
        every = mm(lift, cells).astype(BF)
        own = iota((count * 8, 128), 0) % 8 == iota((count * 8, 128), 1) % 8
        rep = jnp.where(own, every.astype(F32), 0.0).astype(BF)
        occ = mm(rep, sel_o)
        return mm(rep, sel_j) + const_j, occ * BIG_H - BIG_H, mm(every, sel_o), occ, every

    def fill(where, values, shape):
        for table, value in zip((gj_ref, sf_ref, cc_ref), values):
            table[where] = value.reshape(shape)

    for u in range(4):
        at = slice(u * 512, u * 512 + 512)
        gj, mask, number, occ, every = cell_rows(geo_ref[u * 64 : u * 64 + 64], 0, 64)
        cells = slice(8 * u, 8 * u + 8)
        fill((slice(1 + 8 * u, 9 + 8 * u), slice(1, 9)), (gj, mask, number), (8, 8, 8, 128))
        occ_ref[at, :] = occ
        gi_ref[cells] = mm(every, sel_i).reshape(8, 8, 8, 128)
    for copy in first:
        copy.wait()
    for k in DIRECTIONS:
        cat_ref[k * 64 : k * 64 + 64, 0:128] = in_buf[k, 0:64]
    for u in range(4):
        at = slice(u * 512, u * 512 + 512)
        placed = mm(hot_ref[at, :], cat_ref[...])
        rows = lat_ref[at, :].astype(F32) * (1.0 - placed[:, 128:256]) + placed[:, 0:128]
        rel_ref[at, :] = rows.astype(BF)
        cells = rows.reshape(8, 8, 8, 128)
        sy[0, u * 64 : u * 64 + 64] = cells[:, 0].reshape(64, 128).astype(BF)
        sy[1, u * 64 : u * 64 + 64] = cells[:, 7].reshape(64, 128).astype(BF)
        if u == 0:
            sx[0] = rows[0:64].astype(BF)
            sc[0] = rows[0:16].astype(BF)
            sc[1] = rows[48:64].astype(BF)
        if u == 3:
            sx[1] = rows[448:512].astype(BF)
            sc[2] = rows[448:464].astype(BF)
            sc[3] = rows[496:512].astype(BF)
    pairs = ((sx, tx), (sy, ty), (sc, tc))
    second = []
    for k in DIRECTIONS:
        kind, place = rim_slot(k)
        source, target = pairs[kind]
        second.append(send(k, source.at[place], target.at[place], send2, recv2))
    for side in range(2):
        k = 1 if side == 0 else 7
        values = cell_rows(in_buf[k, 64:96], 0 if side == 0 else 24, 8)[:3]
        fill((33 if side == 0 else 0, slice(1, 9)), values, (8, 8, 128))
        k = 3 if side == 0 else 5
        values = cell_rows(in_buf[k, 64:96], 0, 32)[:3]
        fill((slice(1, 33), 9 if side == 0 else 0), values, (32, 8, 128))
    corners = ((0, 0, 33, 9), (2, 7, 33, 0), (6, 24, 0, 9), (8, 31, 0, 0))
    for k, first_row, x, y in corners:
        odd = first_row % 8 != 0
        values = cell_rows(in_buf[k, 64:96], first_row - odd, 2)[:3]
        at = 8 if odd else 0
        fill((x, y), [v[at : at + 8] for v in values], (8, 128))
    for u in range(4):
        rows = rel_ref[u * 512 : u * 512 + 512, :]
        cells = slice(8 * u, 8 * u + 8)
        sf_ref[1 + 8 * u : 9 + 8 * u, 1:9] += mm(rows, sw_half).reshape(8, 8, 8, 128)
        r_ref[cells] = (mm(rows, rw_half) + eb_half).reshape(8, 8, 8, 128)
    for copy in second:
        copy.wait()
    for side in range(2):
        x = 33 if side == 0 else 0
        sf_ref[x, 1:9] += mm(tx[side], sw_half).reshape(8, 8, 128)
        y = 9 if side == 0 else 0
        sf_ref[1:33, y] += mm(ty[side], sw_half).reshape(32, 8, 128)
    for place, (k, first_row, x, y) in enumerate(corners):
        at = 8 if first_row % 8 else 0
        sf_ref[x, y] += mm(tc[place], sw_half)[at : at + 8]

    @pl.loop(0, NH)
    def _(x):
        s_ref[x] = jnp.concatenate([sf_ref[x], sf_ref[x + 16]], axis=1).astype(BF)

    tile = (8, 16, 128)
    blk16 = iota(tile, 2) // 8
    squared = (blk16 >= 6) & (blk16 < 12)
    linear_c = jnp.where(blk16 < 12, blk16 % 3, 3)
    eye = jnp.where((blk16 == 15) & (iota(tile, 2) % 8 == iota(tile, 1) % 8), -BIG_PRE, 0.0)
    def both(ref, x):
        return jnp.concatenate([ref[x], ref[x + 16]], axis=1)

    def spread(rows, p):
        return jnp.concatenate(
            [jnp.broadcast_to(v[:, p : p + 1], (8, 8, 128)) for v in rows], axis=1
        ).reshape(128, 128)

    @pl.loop(0, 16)
    def _(x):
        gi = both(gi_ref, x)
        feats = []
        for n in range(9):
            dx, dy = step_of(n)
            reach = (
                jnp.concatenate(
                    [gj_ref[x + dx, dy : dy + 8], gj_ref[x + 16 + dx, dy : dy + 8]], axis=1
                )
                - gi
            )
            if n != 4:
                reach = reach + jnp.where(
                    linear_c == 0, float(dx - 1), jnp.where(linear_c == 1, float(dy - 1), 0.0)
                )
            value = jnp.where(squared, reach * reach, reach)
            if n == 4:
                value = value + eye
            feats.append(value.reshape(128, 128).astype(BF))
        feats = jnp.concatenate(feats, axis=0)
        own_rows = (r_ref[x], r_ref[x + 16])
        parts = [[], [], []]
        for pp in range(4):
            pre = mm(feats, w1_ref[:, pp * 256 : (pp + 1) * 256])
            enc = jnp.maximum(pre.astype(BF), BF(0))
            hh = mm(enc, bd_ref[...]).astype(BF)
            for half in range(2):
                p = 2 * pp + half
                cols = slice(half * 128, half * 128 + 128)
                r = spread(own_rows, p).astype(BF)
                pieces = [[], [], []]
                for y in range(0, 8, 2):
                    stacks = [[], [], []]
                    inside = slice(y * 16, (y + 2) * 16)
                    for n in range(9):
                        dx, dy = step_of(n)
                        at = slice(n * 128 + y * 16, n * 128 + (y + 2) * 16)
                        near = s_ref[x + dx, dy + y : dy + y + 2].reshape(32, 128)
                        h = hh[at, cols] + (near + r[inside])
                        if n == 4:
                            own = iota((32, 128), 0) % 8 == p
                            h = h + jnp.where(own, -BIG_H, 0.0).astype(BF)
                        t = jnp.tanh(h)
                        q = BF(1) + t
                        silu = h * q
                        slope = q + silu * (BF(1) - t)
                        g_ref[x, p, n, inside] = slope
                        for stack, value in zip(stacks, (enc[at, cols], silu, slope)):
                            stack.append((1, value))
                            while len(stack) > 1 and (stack[-1][0] == stack[-2][0] or n == 8):
                                last, before = stack.pop(), stack.pop()
                                stack.append((last[0] + before[0], last[1] + before[1]))
                    for piece, stack in zip(pieces, stacks):
                        piece.append(stack[0][1])
                for part, piece in zip(parts, pieces):
                    part.append(jnp.concatenate(piece, axis=0))
        beside = [jnp.concatenate(part, axis=0) for part in parts]
        totals = mm(red_ref[...], jnp.concatenate(beside, axis=1))
        for c, out in enumerate((se_ref, sh_ref, sg_ref)):
            total = totals[:, c * 128 : c * 128 + 128]
            at = pl.multiple_of(x * 64, 64)
            out[pl.ds(at, 64), :] = total[:64]
            out[pl.ds(at + 1024, 64), :] = total[64:]

    CH = 512

    @pl.loop(0, 2048 // CH)
    def _(k):
        wide_x = CH // 64
        near_y = cc_ref[pl.ds(k * wide_x, wide_x + 2)]
        near_y = near_y[:, 0:8] + near_y[:, 1:9] + near_y[:, 2:10]
        near = near_y[0:wide_x] + near_y[1 : wide_x + 1] + near_y[2 : wide_x + 2]
        number = near.reshape(CH, 128) - 1.0
        at = pl.ds(pl.multiple_of(k * CH, CH), CH)
        sh = sh_ref[at, :]
        sh_b = sh.astype(BF)
        sh_l = (sh - sh_b.astype(F32)).astype(BF)
        mw = mw_ref[...]
        summed = se_ref[at, :] + mm(sh_b, mw) + mm(sh_l, mw) + number * mb_ref[...]
        inner = mm(rel_ref[at, :], nw_ref[...]) + mm(summed.astype(BF), uw_ref[...]) + nb_ref[...]
        h = inner * 0.5
        t = jnp.tanh(h)
        q = 1.0 + t
        silu = h * q
        dsilu = 0.5 * (q + silu * (1.0 - t))
        output = mm(silu.astype(BF), ow_ref[...]) + ob_ref[...]
        centred = output - jnp.mean(output, axis=-1, keepdims=True)
        inv = lax.rsqrt(jnp.mean(centred * centred, axis=-1, keepdims=True) + ln_eps)
        normed = centred * inv
        occ = occ_ref[at, :]
        gain = gain_ref[...]
        upd_ref[at, :] = (rel_ref[at, :].astype(F32) + occ * normed * gain).astype(BF)
        cot = cot_ref[at, :].astype(F32)
        gn = occ * cot * gain
        go = (
            (
                gn
                - jnp.mean(gn, axis=-1, keepdims=True)
                - normed * jnp.mean(gn * normed, axis=-1, keepdims=True)
            )
            * inv
        ).astype(BF)
        ginner = (mmt(go, ow_ref[...]) * dsilu).astype(BF)
        gsum = mmt(ginner, uw_ref[...]).astype(BF)
        pull = mmt(gsum, mw) * 0.5
        r_ref[pl.ds(k * wide_x, wide_x)] = pull.reshape(wide_x, 8, 8, 128)
        rgrad = (pull * sg_ref[at, :]).astype(BF)
        total = cot + mmt(ginner, nw_ref[...]) + mmt(rgrad, rw_ref[...])
        grad_ref[pl.ds(k * wide_x, wide_x)] = total.reshape(wide_x, 8, 8, 128)


    sf_ref[...] = jnp.zeros(sf_ref.shape, F32)

    def tiles(x, y):
        rows = (r_ref[x, y], r_ref[x + 16, y])
        return [
            jnp.concatenate(
                [jnp.broadcast_to(v[p : p + 1], (8, 128)) for v in rows], axis=0
            )
            for p in range(8)
        ]

    @pl.loop(0, 16)
    def _(x):
        for y in range(8):
            pulls = [v.astype(BF) for v in tiles(x, y)]
            for n in range(9):
                dx, dy = step_of(n)
                total = tree([g_ref[x, p, n, y * 16 : y * 16 + 16] * pulls[p] for p in range(8)])
                total = total.astype(F32)
                sf_ref[x + dx, y + dy] += total[0:8]
                sf_ref[x + 16 + dx, y + dy] += total[8:16]

    for u in range(4):
        for side in range(2):
            edge = sf_ref[1 + 8 * u : 9 + 8 * u, 9 * side].reshape(64, 128)
            by[side, u * 64 : u * 64 + 64] = edge.astype(BF)
    for side in range(2):
        x = 33 * side
        bx[side] = sf_ref[x, 1:9].reshape(64, 128).astype(BF)
        for end in range(2):
            cell = sf_ref[x, 9 * end]
            bc[2 * side + end] = jnp.concatenate([cell, jnp.zeros_like(cell)], axis=0).astype(BF)
    pairs = ((bx, dx_buf), (by, dy_buf), (bc, dc_buf))
    third = []
    for k in DIRECTIONS:
        kind, place = rim_slot(k)
        source, target = pairs[kind]
        third.append(send(k, source.at[place], target.at[place], send3, recv3))
    sw = sw_ref[...]
    for u in range(4):
        core = sf_ref[1 + 8 * u : 9 + 8 * u, 1:9].reshape(512, 128).astype(BF)
        grad_ref[8 * u : 8 * u + 8] += mmt(core, sw).reshape(8, 8, 8, 128)
    for copy in third:
        copy.wait()
    for side in range(2):
        at = 31 if side == 0 else 0
        grad_ref[at] += mmt(dx_buf[side], sw).reshape(8, 8, 128)
        at = 7 if side == 0 else 0
        grad_ref[:, at] += mmt(dy_buf[side], sw).reshape(32, 8, 128)
    corner = mmt(dc_buf[...].reshape(64, 128), sw).reshape(4, 16, 128)[:, 0:8]
    grad_ref[31, 7] += corner[0]
    grad_ref[31, 0] += corner[1]
    grad_ref[0, 7] += corner[2]
    grad_ref[0, 0] += corner[3]


def step_call(*operands):
    full = pl.BlockSpec(memory_space=pltpu.VMEM)
    rim = [(2, 64, 128), (2, 256, 128), (4, 16, 128)]
    return pl.pallas_call(
        step_kernel,
        out_shape=(
            jax.ShapeDtypeStruct((2048, 128), BF),
            jax.ShapeDtypeStruct((32, 8, 8, 128), F32),
        ),
        in_specs=[full] * len(operands),
        out_specs=(full,) * 2,
        scratch_shapes=[pltpu.VMEM((9, 96, 128), BF), pltpu.VMEM((9, 96, 128), BF)]
        + [pltpu.VMEM(v, BF) for v in rim * 4]
        + [
            pltpu.VMEM((2304, 640), BF),
            pltpu.VMEM((640, 256), BF),
            pltpu.VMEM((2048, 128), BF),
            pltpu.VMEM((256, 128), BF),
            pltpu.VMEM((34, 10, 8, 128), F32),
            pltpu.VMEM((32, 8, 8, 128), F32),
            pltpu.VMEM((34, 10, 8, 128), F32),
            pltpu.VMEM((NH, 10, 16, 128), BF),
            pltpu.VMEM((32, 8, 8, 128), F32),
            pltpu.VMEM((2048, 128), F32),
            pltpu.VMEM((34, 10, 8, 128), F32),
            pltpu.VMEM((128, 1024), BF),
            pltpu.VMEM((256, 256), BF),
            pltpu.VMEM((128, 1024), BF),
            pltpu.VMEM((2048, 128), F32),
            pltpu.VMEM((2048, 128), F32),
            pltpu.VMEM((2048, 128), F32),
            pltpu.VMEM((16, 8, 9, 128, 128), BF),
        ]
        + [pltpu.SemaphoreType.DMA((9,))] * 6,
        compiler_params=pltpu.CompilerParams(
            collective_id=0, has_side_effects=True, vmem_limit_bytes=62 * 1024 * 1024
        ),
        name="step",
    )(*operands)


def write_kernel(upd_ref, grad_ref, upd_out, grad_out, upd_held, grad_held, sems_in, sems_out):
    pieces = [(grad_ref, grad_held, grad_out, pl.ds(8 * u, 8)) for u in range(4)]
    pieces += [(upd_ref, upd_held, upd_out, pl.ds(1024 * u, 1024)) for u in range(2)]
    entering = []
    for place, (source, held, _, at) in enumerate(pieces):
        entering.append(pltpu.make_async_copy(source.at[at], held.at[at], sems_in.at[place]))
        entering[-1].start()
    leaving = []
    for place, (_, held, target, at) in enumerate(pieces):
        entering[place].wait()
        leaving.append(pltpu.make_async_copy(held.at[at], target.at[at], sems_out.at[place]))
        leaving[-1].start()
    for copy in leaving:
        copy.wait()


def write_call(updated, grad):
    place = pl.BlockSpec(memory_space=pl.ANY)
    return pl.pallas_call(
        write_kernel,
        out_shape=(
            jax.ShapeDtypeStruct(updated.shape, BF),
            jax.ShapeDtypeStruct(grad.shape, F32),
        ),
        in_specs=[place] * 2,
        out_specs=(place,) * 2,
        scratch_shapes=[
            pltpu.VMEM(updated.shape, BF),
            pltpu.VMEM(grad.shape, F32),
            pltpu.SemaphoreType.DMA((6,)),
            pltpu.SemaphoreType.DMA((6,)),
        ],
        compiler_params=pltpu.CompilerParams(vmem_limit_bytes=60 * 1024 * 1024),
        name="write",
    )(updated, grad)


def on_device(
    latent, position, counts, leaving, landing, cotangent, encoder_weight, encoder_bias,
    receiver_weight, sender_weight, edge_weight, edge_bias, message_weight, message_bias,
    node_weight, summed_weight, node_bias, output_weight, output_bias, norm_gain,
):
    places = jnp.transpose(position, (1, 2, 3, 0)).reshape(8, 24, 32)
    line = lambda v: v.reshape(1, -1)
    updated, grad = step_call(
        latent.reshape(2048, 128), jnp.transpose(leaving, (0, 2, 1, 3)),
        jnp.transpose(landing, (0, 2, 1, 3)), places, jnp.transpose(counts),
        cotangent.reshape(2048, 128), encoder_weight, line(encoder_bias), receiver_weight,
        sender_weight, edge_weight, line(edge_bias), message_weight, line(message_bias),
        node_weight, summed_weight, line(node_bias), output_weight, line(output_bias),
        line(norm_gain),
    )
    updated, grad = write_call(updated, grad)
    return updated.reshape(latent.shape), grad


def solution(mesh):
    split = P("gx", "gy", None, None)
    return jax.shard_map(
        on_device,
        mesh=mesh,
        in_specs=(split, split, P("gx", "gy"), split, split, split) + (P(),) * 14,
        out_specs=(split, split),
        check_vma=False,
    )
```

```python
import jax
import jax.numpy as jnp
from jax import lax
from jax.experimental import pallas as pl
from jax.experimental.pallas import tpu as pltpu
from jax.sharding import PartitionSpec as P

ln_eps = 1e-05
F32 = jnp.float32
BF = jnp.bfloat16
BIG_PRE = 4096.0
BIG_H = 131072.0
NH = 18
MESH = pl.DeviceIdType.MESH
DIRECTIONS = [k for k in range(9) if k != 4]


def mm(a, b):
    return jnp.dot(a, b, preferred_element_type=F32)


def mmt(a, b):
    return lax.dot_general(a, b, (((1,), (1,)), ((), ())), preferred_element_type=F32)


def iota(shape, dim):
    return lax.broadcasted_iota(jnp.int32, shape, dim)


def tree(parts):
    parts = list(parts)
    while len(parts) > 1:
        parts = [
            parts[i] + parts[i + 1] if i + 1 < len(parts) else parts[i]
            for i in range(0, len(parts), 2)
        ]
    return parts[0]


def step_of(n):
    return n // 3, n % 3


def neighbour(k):
    dx, dy = step_of(k)
    nx, ny = lax.axis_size("gx"), lax.axis_size("gy")
    return (
        lax.rem(lax.axis_index("gx") + (dx - 1 + nx), nx),
        lax.rem(lax.axis_index("gy") + (dy - 1 + ny), ny),
    )


def send(k, source, target, send_sem, recv_sem):
    copy = pltpu.make_async_remote_copy(
        src_ref=source, dst_ref=target, send_sem=send_sem.at[k], recv_sem=recv_sem.at[k],
        device_id=neighbour(k), device_id_type=MESH,
    )
    copy.start()
    return copy


def rim_slot(k):
    dx, dy = step_of(k)
    if dy == 1:
        return 0, dx // 2
    if dx == 1:
        return 1, dy // 2
    return 2, dx // 2 * 2 + dy // 2


def step_kernel(
    lat_ref, leave_ref, land_ref, place_ref, count_ref, cot_ref,
    ew_ref, eb_ref, rw_ref, sw_ref, dw_ref, db_ref, mw_ref, mb_ref,
    nw_ref, uw_ref, nb_ref, ow_ref, ob_ref, gain_ref,
    upd_ref, grad_ref,
    out_buf, in_buf, sx, sy, sc, tx, ty, tc, bx, by, bc, dx_buf, dy_buf, dc_buf,
    hot_ref, cat_ref, rel_ref, geo_ref,
    gj_ref, gi_ref, sf_ref, s_ref, r_ref, occ_ref, cc_ref, w1_ref, bd_ref, red_ref,
    se_ref, sh_ref, sg_ref, g_ref,
    send1, recv1, send2, recv2, send3, recv3,
):
    barrier = pltpu.get_barrier_semaphore()
    for k in DIRECTIONS:
        pl.semaphore_signal(barrier, inc=1, device_id=neighbour(k), device_id_type=MESH)
    unit = jnp.where(iota((32, 32), 0) == iota((32, 32), 1), 1.0, 0.0).astype(BF)
    count = count_ref[...].astype(F32)
    turned = []
    for y in range(8):
        held = jnp.where(iota((8, 32), 0).astype(F32) < count[y : y + 1], 1.0, 0.0)
        lanes_x = jnp.concatenate([place_ref[y].astype(F32), held], axis=0).astype(BF)
        turned.append(mmt(unit, lanes_x))
    turned = jnp.concatenate(turned, axis=0).astype(BF)
    cell_row = iota((256, 256), 0)
    order = jnp.where(iota((256, 256), 1) == cell_row % 8 * 32 + cell_row // 8, 1.0, 0.0).astype(BF)
    widen = jnp.where(iota((32, 128), 0) == iota((32, 128), 1), 1.0, 0.0).astype(BF)
    geo_ref[...] = mm(mm(order, turned).astype(BF), widen).astype(BF)
    leave = jnp.concatenate([leave_ref[0, k] for k in range(9)], axis=0)
    upper = jnp.where(leave < 0, -64, leave // 64 * 64)
    lower = (leave - upper).astype(F32)
    upper = upper.astype(F32)
    eye = iota((64, 64), 0) == iota((64, 64), 1)
    ones = jnp.ones((64, 128), BF)
    slots = iota((64, 128), 1).astype(F32)
    for k in range(9):
        column = mm(jnp.where(eye, upper[k : k + 1], 0.0).astype(BF), ones) + mm(
            jnp.where(eye, lower[k : k + 1], 0.0).astype(BF), ones
        )
        for t in range(16):
            row = t // 4 * 576 + k * 64
            hot_ref[row : row + 64, t % 4 * 128 : t % 4 * 128 + 128] = jnp.where(
                column == slots + t * 128.0, 1.0, 0.0
            ).astype(BF)
    picked = tree(
        [
            mm(hot_ref[u * 576 : u * 576 + 576, 0:512], lat_ref[u * 512 : u * 512 + 512, :])
            for u in range(4)
        ]
    ).astype(BF)
    edges = jnp.where(
        iota((64, 256), 1) == iota((64, 256), 0) % 32 * 8 + iota((64, 256), 0) // 32 * 7, 1.0, 0.0
    ).astype(BF)
    geo_y = mm(edges, geo_ref[...]).astype(BF)
    for k in range(9):
        dx, dy = step_of(k)
        out_buf[k, 0:64] = picked[k * 64 : k * 64 + 64]
        if dx == 1 and dy != 1:
            out_buf[k, 64:96] = geo_y[dy // 2 * 32 : dy // 2 * 32 + 32]
        else:
            first = 0 if dx == 0 else 224
            out_buf[k, 64:96] = geo_ref[first : first + 32]
    pl.semaphore_wait(barrier, 8)
    first = [send(k, out_buf.at[k], in_buf.at[k], send1, recv1) for k in DIRECTIONS]
    land = [land_ref[0, k] for k in range(9)]
    for t in range(5):
        if t < 4:
            row = jnp.concatenate([land[2 * t], land[2 * t + 1]], axis=1)
        else:
            row = jnp.concatenate([land[8], jnp.full((1, 64), -1, jnp.int32)], axis=1)
        for u in range(8):
            hot_ref[u * 256 : u * 256 + 256, t * 128 : t * 128 + 128] = jnp.where(
                iota((256, 128), 0) + u * 256 == row, 1.0, 0.0
            ).astype(BF)
    cat_ref[:, 128:256] = jnp.ones((640, 128), BF)
    cat_ref[576:640, 0:128] = jnp.zeros((64, 128), BF)
    cat_ref[256:320, 0:128] = picked[256:320]
    lane = iota((128, 128), 1)
    row = iota((128, 128), 0)
    whole = ew_ref[...]
    high = whole.astype(BF).astype(F32)
    low = whole - high
    bias_high = eb_ref[...].astype(BF).astype(F32)
    bias_low = eb_ref[...] - bias_high
    wide = lambda v: jnp.broadcast_to(v, (8, 128))
    blocks = [wide(high[c : c + 1]) for c in range(3)]
    blocks += [wide(low[c : c + 1]) for c in range(3)]
    blocks += [wide(high[3:4])] * 3 + [wide(low[3:4])] * 3
    blocks += [wide(bias_high), wide(bias_low)]
    blocks += [jnp.ones((16, 128), F32)]
    stacked = jnp.concatenate(blocks, axis=0)
    for p in range(8):
        w1_ref[:, p * 128 : (p + 1) * 128] = jnp.where(row % 8 == p, stacked, 0.0).astype(BF)
    half_w = (dw_ref[...].astype(F32) * 0.5).astype(BF)
    bd_ref[...] = jnp.zeros((256, 256), BF)
    bd_ref[0:128, 0:128] = half_w
    bd_ref[128:256, 128:256] = half_w

    comp = row // 8
    slot = row % 8
    blk = lane // 8
    in_p = lane % 8
    is_pos = blk < 12
    sel_j = jnp.where(
        is_pos & (comp == blk % 3), 1.0, 0.0
    ) + jnp.where((blk == 14) & (comp == 3), BIG_PRE, 0.0)
    sel_j = jnp.where(comp < 4, sel_j, 0.0).astype(BF)
    sel_i = jnp.where(is_pos & (comp == blk % 3) & (slot == in_p), 1.0, 0.0).astype(BF)
    sel_o = jnp.where(comp == 3, 1.0, 0.0).astype(BF)
    const_blk = iota((1, 128), 1) // 8
    const_j = jnp.where((const_blk == 12) | (const_blk == 13), 1.0, 0.0) + jnp.where(
        const_blk == 14, -BIG_PRE, 0.0
    )
    sw_half = (sw_ref[...].astype(F32) * 0.5).astype(BF)
    rw_half = (rw_ref[...].astype(F32) * 0.5).astype(BF)
    eb_half = db_ref[...] * 0.5

    red_row = iota((128, 1024), 0)
    red_col = iota((128, 1024), 1)
    red_ref[...] = jnp.where(
        (red_row // 64 == red_col // 8 % 2)
        & (red_row // 8 % 8 == red_col // 16 % 8)
        & (red_row % 8 == red_col // 128),
        1.0,
        0.0,
    ).astype(BF)

    def cell_rows(cells, offset, count):
        size = cells.shape[0]
        lift = jnp.where(
            iota((count * 8, size), 0) // 8 + offset == iota((count * 8, size), 1), 1.0, 0.0
        ).astype(BF)
        every = mm(lift, cells).astype(BF)
        own = iota((count * 8, 128), 0) % 8 == iota((count * 8, 128), 1) % 8
        rep = jnp.where(own, every.astype(F32), 0.0).astype(BF)
        occ = mm(rep, sel_o)
        return mm(rep, sel_j) + const_j, occ * BIG_H - BIG_H, mm(every, sel_o), occ, every

    def fill(where, values, shape):
        for table, value in zip((gj_ref, sf_ref, cc_ref), values):
            table[where] = value.reshape(shape)

    for u in range(4):
        at = slice(u * 512, u * 512 + 512)
        gj, mask, number, occ, every = cell_rows(geo_ref[u * 64 : u * 64 + 64], 0, 64)
        cells = slice(8 * u, 8 * u + 8)
        fill((slice(1 + 8 * u, 9 + 8 * u), slice(1, 9)), (gj, mask, number), (8, 8, 8, 128))
        occ_ref[at, :] = occ
        gi_ref[cells] = mm(every, sel_i).reshape(8, 8, 8, 128)
    for copy in first:
        copy.wait()
    for k in DIRECTIONS:
        cat_ref[k * 64 : k * 64 + 64, 0:128] = in_buf[k, 0:64]
    for u in range(4):
        at = slice(u * 512, u * 512 + 512)
        placed = mm(hot_ref[at, :], cat_ref[...])
        rows = lat_ref[at, :].astype(F32) * (1.0 - placed[:, 128:256]) + placed[:, 0:128]
        rel_ref[at, :] = rows.astype(BF)
        cells = rows.reshape(8, 8, 8, 128)
        sy[0, u * 64 : u * 64 + 64] = cells[:, 0].reshape(64, 128).astype(BF)
        sy[1, u * 64 : u * 64 + 64] = cells[:, 7].reshape(64, 128).astype(BF)
        if u == 0:
            sx[0] = rows[0:64].astype(BF)
            sc[0] = rows[0:16].astype(BF)
            sc[1] = rows[48:64].astype(BF)
        if u == 3:
            sx[1] = rows[448:512].astype(BF)
            sc[2] = rows[448:464].astype(BF)
            sc[3] = rows[496:512].astype(BF)
    pairs = ((sx, tx), (sy, ty), (sc, tc))
    second = []
    for k in DIRECTIONS:
        kind, place = rim_slot(k)
        source, target = pairs[kind]
        second.append(send(k, source.at[place], target.at[place], send2, recv2))
    for side in range(2):
        k = 1 if side == 0 else 7
        values = cell_rows(in_buf[k, 64:96], 0 if side == 0 else 24, 8)[:3]
        fill((33 if side == 0 else 0, slice(1, 9)), values, (8, 8, 128))
        k = 3 if side == 0 else 5
        values = cell_rows(in_buf[k, 64:96], 0, 32)[:3]
        fill((slice(1, 33), 9 if side == 0 else 0), values, (32, 8, 128))
    corners = ((0, 0, 33, 9), (2, 7, 33, 0), (6, 24, 0, 9), (8, 31, 0, 0))
    for k, first_row, x, y in corners:
        odd = first_row % 8 != 0
        values = cell_rows(in_buf[k, 64:96], first_row - odd, 2)[:3]
        at = 8 if odd else 0
        fill((x, y), [v[at : at + 8] for v in values], (8, 128))
    for u in range(4):
        rows = rel_ref[u * 512 : u * 512 + 512, :]
        cells = slice(8 * u, 8 * u + 8)
        sf_ref[1 + 8 * u : 9 + 8 * u, 1:9] += mm(rows, sw_half).reshape(8, 8, 8, 128)
        r_ref[cells] = (mm(rows, rw_half) + eb_half).reshape(8, 8, 8, 128)
    for copy in second:
        copy.wait()
    for side in range(2):
        x = 33 if side == 0 else 0
        sf_ref[x, 1:9] += mm(tx[side], sw_half).reshape(8, 8, 128)
        y = 9 if side == 0 else 0
        sf_ref[1:33, y] += mm(ty[side], sw_half).reshape(32, 8, 128)
    for place, (k, first_row, x, y) in enumerate(corners):
        at = 8 if first_row % 8 else 0
        sf_ref[x, y] += mm(tc[place], sw_half)[at : at + 8]

    @pl.loop(0, NH)
    def _(x):
        s_ref[x] = jnp.concatenate([sf_ref[x], sf_ref[x + 16]], axis=1).astype(BF)

    tile = (8, 16, 128)
    blk16 = iota(tile, 2) // 8
    squared = (blk16 >= 6) & (blk16 < 12)
    linear_c = jnp.where(blk16 < 12, blk16 % 3, 3)
    eye = jnp.where((blk16 == 15) & (iota(tile, 2) % 8 == iota(tile, 1) % 8), -BIG_PRE, 0.0)
    def both(ref, x):
        return jnp.concatenate([ref[x], ref[x + 16]], axis=1)

    def spread(rows, p):
        return jnp.concatenate(
            [jnp.broadcast_to(v[:, p : p + 1], (8, 8, 128)) for v in rows], axis=1
        ).reshape(128, 128)

    @pl.loop(0, 16)
    def _(x):
        gi = both(gi_ref, x)
        feats = []
        for n in range(9):
            dx, dy = step_of(n)
            reach = (
                jnp.concatenate(
                    [gj_ref[x + dx, dy : dy + 8], gj_ref[x + 16 + dx, dy : dy + 8]], axis=1
                )
                - gi
            )
            if n != 4:
                reach = reach + jnp.where(
                    linear_c == 0, float(dx - 1), jnp.where(linear_c == 1, float(dy - 1), 0.0)
                )
            value = jnp.where(squared, reach * reach, reach)
            if n == 4:
                value = value + eye
            feats.append(value.reshape(128, 128).astype(BF))
        feats = jnp.concatenate(feats, axis=0)
        own_rows = (r_ref[x], r_ref[x + 16])
        parts = [[], [], []]
        for pp in range(4):
            pre = mm(feats, w1_ref[:, pp * 256 : (pp + 1) * 256])
            enc = jnp.maximum(pre.astype(BF), BF(0))
            hh = mm(enc, bd_ref[...]).astype(BF)
            for half in range(2):
                p = 2 * pp + half
                cols = slice(half * 128, half * 128 + 128)
                r = spread(own_rows, p).astype(BF)
                pieces = [[], [], []]
                for y in range(0, 8, 2):
                    stacks = [[], [], []]
                    inside = slice(y * 16, (y + 2) * 16)
                    for n in range(9):
                        dx, dy = step_of(n)
                        at = slice(n * 128 + y * 16, n * 128 + (y + 2) * 16)
                        near = s_ref[x + dx, dy + y : dy + y + 2].reshape(32, 128)
                        h = (hh[at, cols] + near) + r[inside]
                        if n == 4:
                            own = iota((32, 128), 0) % 8 == p
                            h = h + jnp.where(own, -BIG_H, 0.0).astype(BF)
                        t = jnp.tanh(h)
                        q = BF(1) + t
                        silu = h * q
                        slope = q + silu * (BF(1) - t)
                        g_ref[x, p, n, inside] = slope
                        for stack, value in zip(stacks, (enc[at, cols], silu, slope)):
                            stack.append((1, value))
                            while len(stack) > 1 and (stack[-1][0] == stack[-2][0] or n == 8):
                                last, before = stack.pop(), stack.pop()
                                stack.append((last[0] + before[0], last[1] + before[1]))
                    for piece, stack in zip(pieces, stacks):
                        piece.append(stack[0][1])
                for part, piece in zip(parts, pieces):
                    part.append(jnp.concatenate(piece, axis=0))
        beside = [jnp.concatenate(part, axis=0) for part in parts]
        totals = mm(red_ref[...], jnp.concatenate(beside, axis=1))
        for c, out in enumerate((se_ref, sh_ref, sg_ref)):
            total = totals[:, c * 128 : c * 128 + 128]
            at = pl.multiple_of(x * 64, 64)
            out[pl.ds(at, 64), :] = total[:64]
            out[pl.ds(at + 1024, 64), :] = total[64:]

    CH = 1024

    @pl.loop(0, 2048 // CH)
    def _(k):
        wide_x = CH // 64
        near_y = cc_ref[pl.ds(k * wide_x, wide_x + 2)]
        near_y = near_y[:, 0:8] + near_y[:, 1:9] + near_y[:, 2:10]
        near = near_y[0:wide_x] + near_y[1 : wide_x + 1] + near_y[2 : wide_x + 2]
        number = near.reshape(CH, 128) - 1.0
        at = pl.ds(pl.multiple_of(k * CH, CH), CH)
        sh = sh_ref[at, :]
        sh_b = sh.astype(BF)
        sh_l = (sh - sh_b.astype(F32)).astype(BF)
        mw = mw_ref[...]
        summed = se_ref[at, :] + mm(sh_b, mw) + mm(sh_l, mw) + number * mb_ref[...]
        inner = mm(rel_ref[at, :], nw_ref[...]) + mm(summed.astype(BF), uw_ref[...]) + nb_ref[...]
        h = inner * 0.5
        t = jnp.tanh(h)
        q = 1.0 + t
        silu = h * q
        dsilu = 0.5 * (q + silu * (1.0 - t))
        output = mm(silu.astype(BF), ow_ref[...]) + ob_ref[...]
        centred = output - jnp.mean(output, axis=-1, keepdims=True)
        inv = lax.rsqrt(jnp.mean(centred * centred, axis=-1, keepdims=True) + ln_eps)
        normed = centred * inv
        occ = occ_ref[at, :]
        gain = gain_ref[...]
        upd_ref[at, :] = (rel_ref[at, :].astype(F32) + occ * normed * gain).astype(BF)
        cot = cot_ref[at, :].astype(F32)
        gn = occ * cot * gain
        go = (
            (
                gn
                - jnp.mean(gn, axis=-1, keepdims=True)
                - normed * jnp.mean(gn * normed, axis=-1, keepdims=True)
            )
            * inv
        ).astype(BF)
        ginner = (mmt(go, ow_ref[...]) * dsilu).astype(BF)
        gsum = mmt(ginner, uw_ref[...]).astype(BF)
        pull = mmt(gsum, mw) * 0.5
        r_ref[pl.ds(k * wide_x, wide_x)] = pull.reshape(wide_x, 8, 8, 128)
        rgrad = (pull * sg_ref[at, :]).astype(BF)
        total = cot + mmt(ginner, nw_ref[...]) + mmt(rgrad, rw_ref[...])
        grad_ref[pl.ds(k * wide_x, wide_x)] = total.reshape(wide_x, 8, 8, 128)


    sf_ref[...] = jnp.zeros(sf_ref.shape, F32)

    def tiles(x, y):
        rows = (r_ref[x, y], r_ref[x + 16, y])
        return [
            jnp.concatenate(
                [jnp.broadcast_to(v[p : p + 1], (8, 128)) for v in rows], axis=0
            )
            for p in range(8)
        ]

    @pl.loop(0, 16)
    def _(x):
        for y in range(8):
            pulls = [v.astype(BF) for v in tiles(x, y)]
            for n in range(9):
                dx, dy = step_of(n)
                total = tree([g_ref[x, p, n, y * 16 : y * 16 + 16] * pulls[p] for p in range(8)])
                total = total.astype(F32)
                sf_ref[x + dx, y + dy] += total[0:8]
                sf_ref[x + 16 + dx, y + dy] += total[8:16]

    for u in range(4):
        for side in range(2):
            edge = sf_ref[1 + 8 * u : 9 + 8 * u, 9 * side].reshape(64, 128)
            by[side, u * 64 : u * 64 + 64] = edge.astype(BF)
    for side in range(2):
        x = 33 * side
        bx[side] = sf_ref[x, 1:9].reshape(64, 128).astype(BF)
        for end in range(2):
            cell = sf_ref[x, 9 * end]
            bc[2 * side + end] = jnp.concatenate([cell, jnp.zeros_like(cell)], axis=0).astype(BF)
    pairs = ((bx, dx_buf), (by, dy_buf), (bc, dc_buf))
    third = []
    for k in DIRECTIONS:
        kind, place = rim_slot(k)
        source, target = pairs[kind]
        third.append(send(k, source.at[place], target.at[place], send3, recv3))
    sw = sw_ref[...]
    for u in range(4):
        core = sf_ref[1 + 8 * u : 9 + 8 * u, 1:9].reshape(512, 128).astype(BF)
        grad_ref[8 * u : 8 * u + 8] += mmt(core, sw).reshape(8, 8, 8, 128)
    for copy in third:
        copy.wait()
    for side in range(2):
        at = 31 if side == 0 else 0
        grad_ref[at] += mmt(dx_buf[side], sw).reshape(8, 8, 128)
        at = 7 if side == 0 else 0
        grad_ref[:, at] += mmt(dy_buf[side], sw).reshape(32, 8, 128)
    corner = mmt(dc_buf[...].reshape(64, 128), sw).reshape(4, 16, 128)[:, 0:8]
    grad_ref[31, 7] += corner[0]
    grad_ref[31, 0] += corner[1]
    grad_ref[0, 7] += corner[2]
    grad_ref[0, 0] += corner[3]


def step_call(*operands):
    full = pl.BlockSpec(memory_space=pltpu.VMEM)
    rim = [(2, 64, 128), (2, 256, 128), (4, 16, 128)]
    return pl.pallas_call(
        step_kernel,
        out_shape=(
            jax.ShapeDtypeStruct((2048, 128), BF),
            jax.ShapeDtypeStruct((32, 8, 8, 128), F32),
        ),
        in_specs=[full] * len(operands),
        out_specs=(full,) * 2,
        scratch_shapes=[pltpu.VMEM((9, 96, 128), BF), pltpu.VMEM((9, 96, 128), BF)]
        + [pltpu.VMEM(v, BF) for v in rim * 4]
        + [
            pltpu.VMEM((2304, 640), BF),
            pltpu.VMEM((640, 256), BF),
            pltpu.VMEM((2048, 128), BF),
            pltpu.VMEM((256, 128), BF),
            pltpu.VMEM((34, 10, 8, 128), F32),
            pltpu.VMEM((32, 8, 8, 128), F32),
            pltpu.VMEM((34, 10, 8, 128), F32),
            pltpu.VMEM((NH, 10, 16, 128), BF),
            pltpu.VMEM((32, 8, 8, 128), F32),
            pltpu.VMEM((2048, 128), F32),
            pltpu.VMEM((34, 10, 8, 128), F32),
            pltpu.VMEM((128, 1024), BF),
            pltpu.VMEM((256, 256), BF),
            pltpu.VMEM((128, 1024), BF),
            pltpu.VMEM((2048, 128), F32),
            pltpu.VMEM((2048, 128), F32),
            pltpu.VMEM((2048, 128), F32),
            pltpu.VMEM((16, 8, 9, 128, 128), BF),
        ]
        + [pltpu.SemaphoreType.DMA((9,))] * 6,
        compiler_params=pltpu.CompilerParams(
            collective_id=0, has_side_effects=True, vmem_limit_bytes=62 * 1024 * 1024
        ),
        name="step",
    )(*operands)


def write_kernel(upd_ref, grad_ref, upd_out, grad_out, upd_held, grad_held, sems_in, sems_out):
    pieces = [(grad_ref, grad_held, grad_out, pl.ds(8 * u, 8)) for u in range(4)]
    pieces += [(upd_ref, upd_held, upd_out, pl.ds(1024 * u, 1024)) for u in range(2)]
    entering = []
    for place, (source, held, _, at) in enumerate(pieces):
        entering.append(pltpu.make_async_copy(source.at[at], held.at[at], sems_in.at[place]))
        entering[-1].start()
    leaving = []
    for place, (_, held, target, at) in enumerate(pieces):
        entering[place].wait()
        leaving.append(pltpu.make_async_copy(held.at[at], target.at[at], sems_out.at[place]))
        leaving[-1].start()
    for copy in leaving:
        copy.wait()


def write_call(updated, grad):
    place = pl.BlockSpec(memory_space=pl.ANY)
    return pl.pallas_call(
        write_kernel,
        out_shape=(
            jax.ShapeDtypeStruct(updated.shape, BF),
            jax.ShapeDtypeStruct(grad.shape, F32),
        ),
        in_specs=[place] * 2,
        out_specs=(place,) * 2,
        scratch_shapes=[
            pltpu.VMEM(updated.shape, BF),
            pltpu.VMEM(grad.shape, F32),
            pltpu.SemaphoreType.DMA((6,)),
            pltpu.SemaphoreType.DMA((6,)),
        ],
        compiler_params=pltpu.CompilerParams(vmem_limit_bytes=60 * 1024 * 1024),
        name="write",
    )(updated, grad)


def on_device(
    latent, position, counts, leaving, landing, cotangent, encoder_weight, encoder_bias,
    receiver_weight, sender_weight, edge_weight, edge_bias, message_weight, message_bias,
    node_weight, summed_weight, node_bias, output_weight, output_bias, norm_gain,
):
    places = jnp.transpose(position, (1, 2, 3, 0)).reshape(8, 24, 32)
    line = lambda v: v.reshape(1, -1)
    updated, grad = step_call(
        latent.reshape(2048, 128), jnp.transpose(leaving, (0, 2, 1, 3)),
        jnp.transpose(landing, (0, 2, 1, 3)), places, jnp.transpose(counts),
        cotangent.reshape(2048, 128), encoder_weight, line(encoder_bias), receiver_weight,
        sender_weight, edge_weight, line(edge_bias), message_weight, line(message_bias),
        node_weight, summed_weight, line(node_bias), output_weight, line(output_bias),
        line(norm_gain),
    )
    updated, grad = write_call(updated, grad)
    return updated.reshape(latent.shape), grad


def solution(mesh):
    split = P("gx", "gy", None, None)
    return jax.shard_map(
        on_device,
        mesh=mesh,
        in_specs=(split, split, P("gx", "gy"), split, split, split) + (P(),) * 14,
        out_specs=(split, split),
        check_vma=False,
    )
```
